32 devices in a mesh: gx: 4 (over y, x), gy: 8 (over z, core).
Axes of the slice: x: 2, y: 2, z: 4, core: 2. Of those that a mesh axis runs over, the one named last changes fastest.
Arguments:
- old_state: float32 [256, 6, 32768], P(('gx', 'gy')), may hold values from -6 to 6
- old_owner: int32 [128], replicated, may hold values from 0 to 31, as said below
- old_slot: int32 [128], replicated, may hold values from 0 to 7, as said below
- diffusivity: float32 [6], replicated, may hold values from 0.01 to 0.08
Outputs:
- new_state: float32 [128, 6, 32768], P(('gx', 'gy'))
The draws below stay inside these ranges and needn't reach their ends.
Inputs may be any that keep to these rules, and one draw needn't show every extreme that they name: The curve is closed: with n = g // 4 the new owner of box g, old_owner[g] is n, or n - 1 modulo the device count for one of the first 2 boxes of n, or n + 1 modulo the device count for one of the last 2 boxes of n. `old_slot`: A box kept by its owner sits in slot 2 + g % 4; the j-th of the first 2 boxes of a device, when held by the device below, sat in that device's slot 6 + j; the j-th of the last 2 boxes, when held by the device above, sat in its slot j. Slots that hold no box hold anything. Some device takes over 2 boxes from each neighbour in every draw.
All inputs are finite; a program needn't handle non-finite values.
Results may differ from the reference program's by a relative error of at most 0.0003.
Values sent between devices are 32-bit elements; how exact they have to be, the bound alone decides.
A program may use at most 128 MiB of HBM per device.

```python
import math
import jax
import jax.numpy as jnp
from jax import lax

B = 32
F = 6
CAP = 4
DRIFT = 2
OLD_CAP = 8
NBOX = 128
SLOTS = 256
CELLS = 32768
N_GX = 4
N_GY = 8


def owner_and_slot(key):
    devices = NBOX // CAP
    coins = jax.random.randint(jax.random.fold_in(key, 17), (devices, CAP), 0, 2).astype(jnp.int32)
    device = jnp.arange(devices, dtype=jnp.int32)
    forced = (device == 0) | (device == 1) | (device == devices // 2 - 1) | (device == devices // 2) | (device == devices // 2 + 1) | (device == devices - 2) | (device == devices - 1)
    coins = jnp.where(forced[:, None], 1, coins).astype(jnp.int32)
    column = jnp.arange(CAP, dtype=jnp.int32)[None, :]
    owner_home = jnp.broadcast_to(device[:, None], (devices, CAP)).astype(jnp.int32)
    from_below = (column < DRIFT) & (coins == 1)
    from_above = (column >= CAP - DRIFT) & (coins == 1)
    owner = jnp.where(from_below, (owner_home - 1 + devices) % devices, jnp.where(from_above, (owner_home + 1) % devices, owner_home))
    kept_slot = jnp.broadcast_to(DRIFT + column, (devices, CAP))
    slot = jnp.where(from_below, OLD_CAP - DRIFT + column, jnp.where(from_above, column - (CAP - DRIFT), kept_slot))
    return (owner.reshape(NBOX).astype(jnp.int32), slot.reshape(NBOX).astype(jnp.int32))


def draw_old_owner(key, part):
    return owner_and_slot(key)[0]


def draw_old_slot(key, part):
    return owner_and_slot(key)[1]


def levels(stream_key, dims, split, smallest, top_value):
    level = 1.0
    for dim, parts in split:
        heights = jax.random.uniform(jax.random.fold_in(jax.random.fold_in(stream_key, 6), dim), (parts,), jnp.float32, smallest / len(split), top_value / len(split))
        level = level * jnp.repeat(jnp.exp(heights), dims[dim] // parts).reshape((-1,) + (1,) * (len(dims) - 1 - dim))
    return level


def gaussian(rng, shape, scale, most, pieces=(), kind=jnp.bfloat16):
    gain = levels(rng, shape, pieces, -0.22, 0.18) if pieces else 1.0
    result = jax.random.normal(rng, shape, jnp.float32) * scale * gain
    return jnp.minimum(jnp.maximum(result, -most), most).astype(kind)


def setup_inputs(seed: int = 0) -> dict:
    splits = jax.random.split(jax.random.key(seed), 5)
    old_state = gaussian(splits[0], (SLOTS, F, CELLS), 1.0, 6.0, ((0, 32),), jnp.float32)
    old_owner = draw_old_owner(jax.random.fold_in(splits[4], 71), 0)
    old_slot = draw_old_slot(jax.random.fold_in(splits[4], 71), 0)
    diffusivity = jnp.clip(jnp.exp(jax.random.uniform(splits[3], (F,), jnp.float32, math.log(0.01), math.log(0.08))), 0.01, 0.08)
    return dict(old_state=old_state, old_owner=old_owner, old_slot=old_slot, diffusivity=diffusivity)


courant = 0.25


def minmod(former, latter):
    return 0.5 * (jnp.sign(former) + jnp.sign(latter)) * jnp.minimum(jnp.abs(former), jnp.abs(latter))


def part_of(values, bottom, ceiling, dimension):
    return lax.slice_in_dim(values, bottom, ceiling, axis=dimension)


def along(stripe, dimension, velocity_index, spread):
    length = stripe.shape[dimension]
    differ = part_of(stripe, 1, length, dimension) - part_of(stripe, 0, length - 1, dimension)
    slopes = minmod(part_of(differ, 0, length - 2, dimension), part_of(differ, 1, length - 1, dimension))
    left_side = part_of(stripe, 1, length - 2, dimension) + 0.5 * part_of(slopes, 0, length - 3, dimension)
    rights = part_of(stripe, 2, length - 1, dimension) - 0.5 * part_of(slopes, 1, length - 2, dimension)
    velocity = stripe[velocity_index:velocity_index + 1]
    face_speed = 0.5 * (part_of(velocity, 1, length - 2, dimension) + part_of(velocity, 2, length - 1, dimension))
    conduct = jnp.exp(0.5 * jnp.tanh(stripe[5:6]))
    face_conduct = 0.5 * (part_of(conduct, 1, length - 2, dimension) + part_of(conduct, 2, length - 1, dimension))
    fluxes = jnp.maximum(face_speed, 0.0) * left_side + jnp.minimum(face_speed, 0.0) * rights
    gradient = spread * face_conduct * part_of(differ, 1, length - 2, dimension)
    net_flux = gradient - courant * fluxes
    return part_of(net_flux, 1, length - 3, dimension) - part_of(net_flux, 0, length - 4, dimension)


def advance(zstripe, ystripe, xstripe, diffusivity):
    spread = diffusivity.reshape(-1, 1, 1, 1)
    center = part_of(xstripe, 2, xstripe.shape[3] - 2, 3)
    total = center + along(zstripe, 1, 2, spread)
    total = total + along(ystripe, 2, 1, spread)
    return total + along(xstripe, 3, 0, spread)


def reference(old_state, old_owner, old_slot, diffusivity):
    rows = (old_owner * OLD_CAP + old_slot).astype(jnp.int32)
    gathered = old_state[rows]
    domain = gathered.reshape(N_GX, N_GY, CAP, F, B, B, B).transpose(3, 0, 4, 1, 5, 2, 6)
    domain = domain.reshape(F, N_GX * B, N_GY * B, CAP * B)
    padded = jnp.pad(domain, ((0, 0), (2, 2), (2, 2), (2, 2)), mode="edge")

    def advance_device(device):
        row_z = ((device // N_GY) * B).astype(jnp.int32)
        row_y = ((device % N_GY) * B).astype(jnp.int32)
        window = lax.dynamic_slice(padded, (jnp.int32(0), row_z, row_y, jnp.int32(0)), (F, B + 4, B + 4, CAP * B + 4))
        return advance(window[:, :, 2:-2, 2:-2], window[:, 2:-2, :, 2:-2], window[:, 2:-2, 2:-2, :], diffusivity)

    updated = lax.map(advance_device, jnp.arange(N_GX * N_GY, dtype=jnp.int32))
    updated = updated.reshape(N_GX * N_GY, F, B, B, CAP, B).transpose(0, 4, 1, 2, 3, 5)
    return updated.reshape(NBOX, F, B * B * B)
```

```python
import jax
import jax.numpy as jnp
from jax import lax
from jax.experimental import pallas as pl
from jax.experimental.pallas import tpu as pltpu
from jax.sharding import PartitionSpec as P

F = 6
CAP = 4
CHUNKS = 8
TILES = 8
PLANE = 1024
MESH = pl.DeviceIdType.MESH


def kernel(
    n_gx, n_gy, owner_ref, diff_ref, state_ref, out_ref,
    held, send, recv, q, cond, acc, wz, cz, wy, cy, wx, cx,
    zsend, zrecv, ysend, yrecv,
    in_sem, move_send, move_recv, z_send, z_recv, y_send, y_recv,
):
    gx = lax.axis_index("gx")
    gy = lax.axis_index("gy")
    count = n_gx * n_gy
    me = gx * n_gy + gy
    above = lax.rem(me + 1, count)
    below = lax.rem(me + count - 1, count)
    ring = ((above // n_gy, lax.rem(above, n_gy)), (below // n_gy, lax.rem(below, n_gy)))

    def in_copy(k, part):
        cells = pl.ds(pl.multiple_of((k + 8 * part) * PLANE, PLANE), PLANE)
        return pltpu.make_async_copy(
            state_ref.at[:, :, cells], held.at[:, :, cells], in_sem.at[k, part]
        )

    def start_in(k, _):
        for part in range(4):
            in_copy(k, part).start()
        return 0

    lax.fori_loop(0, CHUNKS, start_in, 0)

    barrier = pltpu.get_barrier_semaphore()
    for target in ring:
        pl.semaphore_signal(barrier, inc=1, device_id=target, device_id_type=MESH)

    @pl.when(gx > 0)
    def _():
        pl.semaphore_signal(barrier, inc=1, device_id=(gx - 1, gy), device_id_type=MESH)

    @pl.when(gx < n_gx - 1)
    def _():
        pl.semaphore_signal(barrier, inc=1, device_id=(gx + 1, gy), device_id_type=MESH)

    pl.semaphore_wait(
        barrier, 2 + (gx > 0).astype(jnp.int32) + (gx < n_gx - 1).astype(jnp.int32)
    )

    row = lax.broadcasted_iota(jnp.int32, (8, 128), 0)
    lane = lax.broadcasted_iota(jnp.int32, (8, 128), 1)
    box = row % 4
    col = lane % 32

    def sub(values, shift):
        return pltpu.roll(values, shift % 8, 0)

    def turn(values, shift):
        return pltpu.roll(values, shift % 128, 1)

    def tile_of(f, k, part, t):
        start = pl.multiple_of((k + 8 * part) * PLANE + t * 128, 128)
        return held[f, :, pl.ds(start, 128)]

    def move(way, k):
        return pltpu.make_async_remote_copy(
            src_ref=send.at[way, k],
            dst_ref=recv.at[way, k],
            send_sem=move_send.at[way, k],
            recv_sem=move_recv.at[way, k],
            device_id=ring[way],
            device_id_type=MESH,
        )

    def pack(k, _):
        for part in range(4):
            in_copy(k, part).wait()

        def field(f, _):
            for t in range(TILES):
                a, b, c, d = (tile_of(f, k, part, t) for part in range(4))
                a2, c6 = sub(a, 2), sub(c, 6)
                up = jnp.where(
                    row < 4, jnp.where(row < 2, a2, sub(b, 4)), jnp.where(row < 6, c6, d)
                )
                down = jnp.where(
                    row < 4, jnp.where(row < 2, b, a2), jnp.where(row < 6, sub(d, 4), c6)
                )
                send[0, k, f, t] = up
                send[1, k, f, t] = down
            return 0

        lax.fori_loop(0, F, field, 0)
        move(0, k).start()
        move(1, k).start()
        return 0

    lax.fori_loop(0, CHUNKS, pack, 0)

    owners = jnp.zeros((8, 128), jnp.int32)
    for c in range(CAP):
        owners = jnp.where(box == c, owner_ref[me * CAP + c], owners)
    kept = owners == me

    def y_copy(way, k):
        return pltpu.make_async_remote_copy(
            src_ref=ysend.at[way, k],
            dst_ref=yrecv.at[way, k],
            send_sem=y_send.at[way, k],
            recv_sem=y_recv.at[way, k],
            device_id=(gx, gy + 1) if way == 0 else (gx, gy - 1),
            device_id_type=MESH,
        )

    def z_copy(way):
        return pltpu.make_async_remote_copy(
            src_ref=zsend.at[way],
            dst_ref=zrecv.at[way],
            send_sem=z_send.at[way],
            recv_sem=z_recv.at[way],
            device_id=(gx + 1, gy) if way == 0 else (gx - 1, gy),
            device_id_type=MESH,
        )

    def gather(k, _):
        move(0, k).wait_recv()
        move(1, k).wait_recv()

        def field(f, _):
            for t in range(TILES):
                a, b, c, d = (tile_of(f, k, part, t) for part in range(4))
                up = recv[0, k, f, t]
                down = recv[1, k, f, t]
                first = jnp.where(
                    kept,
                    jnp.where(row < 4, sub(a, 6), sub(c, 2)),
                    jnp.where(box < 2, up, down),
                )
                second = jnp.where(
                    kept,
                    jnp.where(row < 4, sub(b, 6), sub(d, 2)),
                    jnp.where(box < 2, sub(up, 6), sub(down, 2)),
                )
                q[f, k + 2, t + 1] = first
                q[f, k + 10, t + 1] = second
                if t == 0:
                    ysend[1, k, f] = jnp.where(lane < 64, first, turn(second, 64))
                if t == TILES - 1:
                    ysend[0, k, f] = jnp.where(lane < 64, turn(second, 64), first)
            return 0

        lax.fori_loop(0, F, field, 0)

        @pl.when(gy < n_gy - 1)
        def _():
            y_copy(0, k).start()

        @pl.when(gy > 0)
        def _():
            y_copy(1, k).start()

        return 0

    lax.fori_loop(0, CHUNKS, gather, 0)

    def pack_z(f, _):
        for t in range(1, TILES + 1):
            zsend[1, f, t - 1] = jnp.where(row < 4, q[f, 2, t], sub(q[f, 3, t], 4))
            zsend[0, f, t - 1] = jnp.where(row < 4, sub(q[f, 16, t], 4), q[f, 17, t])
        return 0

    lax.fori_loop(0, F, pack_z, 0)

    @pl.when(gx < n_gx - 1)
    def _():
        z_copy(0).start()

    @pl.when(gx > 0)
    def _():
        z_copy(1).start()

    def fill_y(k, _):
        @pl.when(gy > 0)
        def _():
            y_copy(0, k).wait_recv()

        @pl.when(gy < n_gy - 1)
        def _():
            y_copy(1, k).wait_recv()

        def field(f, _):
            lower = yrecv[0, k, f]
            upper = yrecv[1, k, f]
            for plane, low, high in (
                (k + 2, lower, upper), (k + 10, turn(lower, 64), turn(upper, 64))
            ):
                bottom = q[f, plane, 1]
                top = q[f, plane, TILES]
                q[f, plane, 0] = jnp.where(
                    gy == 0, jnp.where(lane < 96, turn(bottom, 64), turn(bottom, 96)), low
                )
                q[f, plane, TILES + 1] = jnp.where(
                    gy == n_gy - 1, jnp.where(lane < 32, turn(top, 32), turn(top, 64)), high
                )
            return 0

        lax.fori_loop(0, F, field, 0)
        return 0

    lax.fori_loop(0, CHUNKS, fill_y, 0)

    @pl.when(gx > 0)
    def _():
        z_copy(0).wait_recv()

    @pl.when(gx < n_gx - 1)
    def _():
        z_copy(1).wait_recv()

    def fill_z(f, _):
        for t in range(1, TILES + 1):
            lower = zrecv[0, f, t - 1]
            upper = zrecv[1, f, t - 1]
            z0, z1, z14, z15 = q[f, 2, t], q[f, 3, t], q[f, 16, t], q[f, 17, t]
            first = gx == 0
            last = gx == n_gx - 1
            q[f, 0, t] = jnp.where(row < 4, jnp.where(first, z0, lower), sub(z14, 4))
            q[f, 1, t] = jnp.where(row < 4, jnp.where(first, z0, sub(lower, 4)), sub(z15, 4))
            q[f, 18, t] = jnp.where(row < 4, sub(z0, 4), jnp.where(last, z15, sub(upper, 4)))
            q[f, 19, t] = jnp.where(row < 4, sub(z1, 4), jnp.where(last, z15, upper))
        return 0

    lax.fori_loop(0, F, fill_z, 0)

    def conduct(z, _):
        for t in range(TILES + 2):
            cond[z, t] = 0.5 * jnp.exp(0.5 * jnp.tanh(q[5, z, t]))
        return 0

    lax.fori_loop(1, 19, conduct, 0)

    def minmod(a, b):
        return jnp.maximum(jnp.minimum(a, b), jnp.minimum(jnp.maximum(a, b), 0.0))

    def face(w, c, spread, d, left, right):
        return spread * c * d - w * jnp.where(w > 0.0, left, right)

    def along_z(t, _):
        for i in range(17):
            wz[i] = 0.125 * (q[2, i + 1, t] + q[2, i + 2, t])
            cz[i] = cond[i + 1, t] + cond[i + 2, t]

        def field(f, _):
            spread = diff_ref[f]
            here = q[f, 1, t]
            d_low = here - q[f, 0, t]
            after = q[f, 2, t]
            d = after - here
            left = here + 0.5 * minmod(d_low, d)
            before = None
            for i in range(17):
                here = after
                after = q[f, i + 3, t]
                d_next = after - here
                half = 0.5 * minmod(d, d_next)
                net = face(wz[i], cz[i], spread, d, left, here - half)
                left = here + half
                d = d_next
                if i > 0:
                    acc[f, i - 1, t - 1] = base + (net - before)
                before = net
                base = here
            return 0

        lax.fori_loop(0, F, field, 0)
        return 0

    lax.fori_loop(1, TILES + 1, along_z, 0)

    edge_low = (box == 0) & (col == 0)
    edge_high = (box == 3) & (col == 31)

    def x_next(values):
        return jnp.where(col == 31, sub(turn(values, 31), -1), turn(values, -1))

    def x_back(values):
        return jnp.where(col == 0, sub(turn(values, -31), 1), turn(values, 1))

    def y_next(values, later):
        return turn(jnp.where(lane < 32, later, values), -32)

    def y_back(values, earlier):
        return turn(jnp.where(lane >= 96, earlier, values), 32)

    def along_yx(z, _):
        for t in range(TILES + 1):
            u, c = q[1, z, t], cond[z, t]
            wy[t] = 0.125 * (u + y_next(u, q[1, z, t + 1]))
            cy[t] = c + y_next(c, cond[z, t + 1])
        for t in range(1, TILES + 1):
            u, c = q[0, z, t], cond[z, t]
            wx[t] = 0.125 * (u + jnp.where(edge_high, u, x_next(u)))
            cx[t] = c + jnp.where(edge_high, c, x_next(c))

        def field(f, _):
            spread = diff_ref[f]
            vals = [q[f, z, t] for t in range(TILES + 2)]
            diffs = [
                y_next(vals[t], vals[min(t + 1, TILES + 1)]) - vals[t] for t in range(TILES + 2)
            ]
            halves = [
                0.5 * minmod(y_back(diffs[t], diffs[max(t - 1, 0)]), diffs[t])
                for t in range(TILES + 2)
            ]
            rights = [v - h for v, h in zip(vals, halves)]
            nets = [
                face(
                    wy[t], cy[t], spread, diffs[t], vals[t] + halves[t],
                    y_next(rights[t], rights[t + 1]),
                )
                for t in range(TILES + 1)
            ]
            for t in range(1, TILES + 1):
                total = acc[f, z - 2, t - 1] + (nets[t] - y_back(nets[t], nets[t - 1]))
                v = vals[t]
                d = jnp.where(edge_high, 0.0, x_next(v) - v)
                half = 0.5 * minmod(jnp.where(edge_low, 0.0, x_back(d)), d)
                right = jnp.where(edge_high, v, x_next(v - half))
                net = face(wx[t], cx[t], spread, d, v + half, right)
                low = jnp.where(edge_low, -0.25 * q[0, z, t] * v, x_back(net))
                total = total + (net - low)
                start = pl.multiple_of((z - 2) * PLANE + (t - 1) * 128, 128)
                out_ref[f, :, pl.ds(start, 128)] = total[:4]
                out_ref[f, :, pl.ds(start + 16 * PLANE, 128)] = total[4:]
            return 0

        lax.fori_loop(0, F, field, 0)
        return 0

    lax.fori_loop(2, 18, along_yx, 0)

    def finish(k, _):
        move(0, k).wait_send()
        move(1, k).wait_send()

        @pl.when(gy < n_gy - 1)
        def _():
            y_copy(0, k).wait_send()

        @pl.when(gy > 0)
        def _():
            y_copy(1, k).wait_send()

        return 0

    lax.fori_loop(0, CHUNKS, finish, 0)

    @pl.when(gx < n_gx - 1)
    def _():
        z_copy(0).wait_send()

    @pl.when(gx > 0)
    def _():
        z_copy(1).wait_send()


def solution(mesh):
    n_gx, n_gy = mesh.shape["gx"], mesh.shape["gy"]

    def local(old_state, old_owner, old_slot, diffusivity):
        def body(*refs):
            kernel(n_gx, n_gy, *refs)

        vmem = pltpu.VMEM
        dma = pltpu.SemaphoreType.DMA
        cells = old_state.shape[2]
        result = pl.pallas_call(
            body,
            out_shape=jax.ShapeDtypeStruct((F, CAP, cells), jnp.float32),
            in_specs=[
                pl.BlockSpec(memory_space=pltpu.SMEM),
                pl.BlockSpec(memory_space=pltpu.SMEM),
                pl.BlockSpec(memory_space=pl.ANY),
            ],
            out_specs=pl.BlockSpec(memory_space=pltpu.VMEM),
            scratch_shapes=[
                vmem((F, 8, cells), jnp.float32),
                vmem((2, CHUNKS, F, TILES, 8, 128), jnp.float32),
                vmem((2, CHUNKS, F, TILES, 8, 128), jnp.float32),
                vmem((F, 20, TILES + 2, 8, 128), jnp.float32),
                vmem((20, TILES + 2, 8, 128), jnp.float32),
                vmem((F, 16, TILES, 8, 128), jnp.float32),
                vmem((17, 8, 128), jnp.float32),
                vmem((17, 8, 128), jnp.float32),
                vmem((TILES + 2, 8, 128), jnp.float32),
                vmem((TILES + 2, 8, 128), jnp.float32),
                vmem((TILES + 2, 8, 128), jnp.float32),
                vmem((TILES + 2, 8, 128), jnp.float32),
                vmem((2, F, TILES, 8, 128), jnp.float32),
                vmem((2, F, TILES, 8, 128), jnp.float32),
                vmem((2, CHUNKS, F, 8, 128), jnp.float32),
                vmem((2, CHUNKS, F, 8, 128), jnp.float32),
                dma((CHUNKS, 4)),
                dma((2, CHUNKS)),
                dma((2, CHUNKS)),
                dma((2,)),
                dma((2,)),
                dma((2, CHUNKS)),
                dma((2, CHUNKS)),
            ],
            compiler_params=pltpu.CompilerParams(
                collective_id=0, has_side_effects=True, vmem_limit_bytes=56 * 2**20
            ),
        )(old_owner, diffusivity, jnp.transpose(old_state, (1, 0, 2)))
        return jnp.transpose(result, (1, 0, 2))

    placed = (P(("gx", "gy"), None, None), P(), P(), P())
    return jax.shard_map(
        local, mesh=mesh, in_specs=placed, out_specs=P(("gx", "gy"), None, None), check_vma=False
    )
```

```python
import jax
import jax.numpy as jnp
from jax import lax
from jax.experimental import pallas as pl
from jax.experimental.pallas import tpu as pltpu
from jax.sharding import PartitionSpec as P

F = 6
CAP = 4
CHUNKS = 8
TILES = 8
PLANE = 1024
MESH = pl.DeviceIdType.MESH


def kernel(
    n_gx, n_gy, owner_ref, diff_ref, state_ref, out_ref,
    held, send, recv, q, cond, acc, wz, cz, wy, cy, wx, cx,
    zsend, zrecv, ysend, yrecv,
    in_sem, move_send, move_recv, z_send, z_recv, y_send, y_recv,
):
    gx = lax.axis_index("gx")
    gy = lax.axis_index("gy")
    count = n_gx * n_gy
    me = gx * n_gy + gy
    above = lax.rem(me + 1, count)
    below = lax.rem(me + count - 1, count)
    ring = ((above // n_gy, lax.rem(above, n_gy)), (below // n_gy, lax.rem(below, n_gy)))

    def in_copy(k, part):
        cells = pl.ds(pl.multiple_of((k + 8 * part) * PLANE, PLANE), PLANE)
        return pltpu.make_async_copy(
            state_ref.at[:, :, cells], held.at[:, :, cells], in_sem.at[k, part]
        )

    def start_in(k, _):
        for part in range(4):
            in_copy(k, part).start()
        return 0

    lax.fori_loop(0, CHUNKS, start_in, 0)

    barrier = pltpu.get_barrier_semaphore()
    for target in ring:
        pl.semaphore_signal(barrier, inc=1, device_id=target, device_id_type=MESH)

    @pl.when(gx > 0)
    def _():
        pl.semaphore_signal(barrier, inc=1, device_id=(gx - 1, gy), device_id_type=MESH)

    @pl.when(gx < n_gx - 1)
    def _():
        pl.semaphore_signal(barrier, inc=1, device_id=(gx + 1, gy), device_id_type=MESH)

    pl.semaphore_wait(
        barrier, 2 + (gx > 0).astype(jnp.int32) + (gx < n_gx - 1).astype(jnp.int32)
    )

    row = lax.broadcasted_iota(jnp.int32, (8, 128), 0)
    lane = lax.broadcasted_iota(jnp.int32, (8, 128), 1)
    box = row % 4
    col = lane % 32

    def sub(values, shift):
        return pltpu.roll(values, shift % 8, 0)

    def turn(values, shift):
        return pltpu.roll(values, shift % 128, 1)

    def tile_of(f, k, part, t):
        start = pl.multiple_of((k + 8 * part) * PLANE + t * 128, 128)
        return held[f, :, pl.ds(start, 128)]

    def move(way, k):
        return pltpu.make_async_remote_copy(
            src_ref=send.at[way, k],
            dst_ref=recv.at[way, k],
            send_sem=move_send.at[way, k],
            recv_sem=move_recv.at[way, k],
            device_id=ring[way],
            device_id_type=MESH,
        )

    def pack(k, _):
        for part in range(4):
            in_copy(k, part).wait()

        def field(f, _):
            for t in range(TILES):
                a, b, c, d = (tile_of(f, k, part, t) for part in range(4))
                a2, c6 = sub(a, 2), sub(c, 6)
                up = jnp.where(
                    row < 4, jnp.where(row < 2, a2, sub(b, 4)), jnp.where(row < 6, c6, d)
                )
                down = jnp.where(
                    row < 4, jnp.where(row < 2, b, a2), jnp.where(row < 6, sub(d, 4), c6)
                )
                send[0, k, f, t] = up
                send[1, k, f, t] = down
            return 0

        lax.fori_loop(0, F, field, 0)
        move(0, k).start()
        move(1, k).start()
        return 0

    lax.fori_loop(0, CHUNKS, pack, 0)

    owners = jnp.zeros((8, 128), jnp.int32)
    for c in range(CAP):
        owners = jnp.where(box == c, owner_ref[me * CAP + c], owners)
    kept = owners == me

    def y_copy(way, k):
        return pltpu.make_async_remote_copy(
            src_ref=ysend.at[way, k],
            dst_ref=yrecv.at[way, k],
            send_sem=y_send.at[way, k],
            recv_sem=y_recv.at[way, k],
            device_id=(gx, gy + 1) if way == 0 else (gx, gy - 1),
            device_id_type=MESH,
        )

    def z_copy(way):
        return pltpu.make_async_remote_copy(
            src_ref=zsend.at[way],
            dst_ref=zrecv.at[way],
            send_sem=z_send.at[way],
            recv_sem=z_recv.at[way],
            device_id=(gx + 1, gy) if way == 0 else (gx - 1, gy),
            device_id_type=MESH,
        )

    def gather(k):
        move(0, k).wait_recv()
        move(1, k).wait_recv()

        def field(f, _):
            for t in range(TILES):
                a, b, c, d = (tile_of(f, k, part, t) for part in range(4))
                up = recv[0, k, f, t]
                down = recv[1, k, f, t]
                first = jnp.where(
                    kept,
                    jnp.where(row < 4, sub(a, 6), sub(c, 2)),
                    jnp.where(box < 2, up, down),
                )
                second = jnp.where(
                    kept,
                    jnp.where(row < 4, sub(b, 6), sub(d, 2)),
                    jnp.where(box < 2, sub(up, 6), sub(down, 2)),
                )
                q[f, k + 2, t + 1] = first
                q[f, k + 10, t + 1] = second
                if t == 0:
                    ysend[1, k, f] = jnp.where(lane < 64, first, turn(second, 64))
                if t == TILES - 1:
                    ysend[0, k, f] = jnp.where(lane < 64, turn(second, 64), first)
            return 0

        lax.fori_loop(0, F, field, 0)

        @pl.when(gy < n_gy - 1)
        def _():
            y_copy(0, k).start()

        @pl.when(gy > 0)
        def _():
            y_copy(1, k).start()

    def fill_y(k):
        @pl.when(gy > 0)
        def _():
            y_copy(0, k).wait_recv()

        @pl.when(gy < n_gy - 1)
        def _():
            y_copy(1, k).wait_recv()

        def field(f, _):
            lower = yrecv[0, k, f]
            upper = yrecv[1, k, f]
            for plane, low, high in (
                (k + 2, lower, upper), (k + 10, turn(lower, 64), turn(upper, 64))
            ):
                bottom = q[f, plane, 1]
                top = q[f, plane, TILES]
                q[f, plane, 0] = jnp.where(
                    gy == 0, jnp.where(lane < 96, turn(bottom, 64), turn(bottom, 96)), low
                )
                q[f, plane, TILES + 1] = jnp.where(
                    gy == n_gy - 1, jnp.where(lane < 32, turn(top, 32), turn(top, 64)), high
                )
            return 0

        lax.fori_loop(0, F, field, 0)

    def conduct(z):
        for t in range(TILES + 2):
            cond[z, t] = 0.5 * jnp.exp(0.5 * jnp.tanh(q[5, z, t]))

    def minmod(a, b):
        return jnp.maximum(jnp.minimum(a, b), jnp.minimum(jnp.maximum(a, b), 0.0))

    def face(w, c, spread, d, left, right):
        return spread * c * d - w * jnp.where(w > 0.0, left, right)

    edge_low = (box == 0) & (col == 0)
    edge_high = (box == 3) & (col == 31)

    def x_next(values):
        return jnp.where(col == 31, sub(turn(values, 31), -1), turn(values, -1))

    def x_back(values):
        return jnp.where(col == 0, sub(turn(values, -31), 1), turn(values, 1))

    def y_next(values, later):
        return turn(jnp.where(lane < 32, later, values), -32)

    def y_back(values, earlier):
        return turn(jnp.where(lane >= 96, earlier, values), 32)

    def along_yx(z):
        conduct(z)
        for t in range(TILES + 1):
            u, c = q[1, z, t], cond[z, t]
            wy[t] = 0.125 * (u + y_next(u, q[1, z, t + 1]))
            cy[t] = c + y_next(c, cond[z, t + 1])
        for t in range(1, TILES + 1):
            u, c = q[0, z, t], cond[z, t]
            wx[t] = 0.125 * (u + jnp.where(edge_high, u, x_next(u)))
            cx[t] = c + jnp.where(edge_high, c, x_next(c))

        def field(f, _):
            spread = diff_ref[f]
            vals = [q[f, z, t] for t in range(TILES + 2)]
            diffs = [
                y_next(vals[t], vals[min(t + 1, TILES + 1)]) - vals[t] for t in range(TILES + 2)
            ]
            halves = [
                0.5 * minmod(y_back(diffs[t], diffs[max(t - 1, 0)]), diffs[t])
                for t in range(TILES + 2)
            ]
            rights = [v - h for v, h in zip(vals, halves)]
            nets = [
                face(
                    wy[t], cy[t], spread, diffs[t], vals[t] + halves[t],
                    y_next(rights[t], rights[t + 1]),
                )
                for t in range(TILES + 1)
            ]
            for t in range(1, TILES + 1):
                total = vals[t] + (nets[t] - y_back(nets[t], nets[t - 1]))
                v = vals[t]
                d = jnp.where(edge_high, 0.0, x_next(v) - v)
                half = 0.5 * minmod(jnp.where(edge_low, 0.0, x_back(d)), d)
                right = jnp.where(edge_high, v, x_next(v - half))
                net = face(wx[t], cx[t], spread, d, v + half, right)
                low = jnp.where(edge_low, -0.25 * q[0, z, t] * v, x_back(net))
                total = total + (net - low)
                acc[f, z - 2, t - 1] = total
            return 0

        lax.fori_loop(0, F, field, 0)

    def update(k):
        fill_y(k)
        along_yx(k + 2)
        along_yx(k + 10)

    def step(k, _):
        gather(k)
        update(k - 1)
        return 0

    gather(0)
    lax.fori_loop(1, CHUNKS, step, 0)

    def pack_z(f, _):
        for t in range(1, TILES + 1):
            zsend[1, f, t - 1] = jnp.where(row < 4, q[f, 2, t], sub(q[f, 3, t], 4))
            zsend[0, f, t - 1] = jnp.where(row < 4, sub(q[f, 16, t], 4), q[f, 17, t])
        return 0

    lax.fori_loop(0, F, pack_z, 0)

    @pl.when(gx < n_gx - 1)
    def _():
        z_copy(0).start()

    @pl.when(gx > 0)
    def _():
        z_copy(1).start()

    update(CHUNKS - 1)

    @pl.when(gx > 0)
    def _():
        z_copy(0).wait_recv()

    @pl.when(gx < n_gx - 1)
    def _():
        z_copy(1).wait_recv()

    def fill_z(f, _):
        for t in range(1, TILES + 1):
            lower = zrecv[0, f, t - 1]
            upper = zrecv[1, f, t - 1]
            z0, z1, z14, z15 = q[f, 2, t], q[f, 3, t], q[f, 16, t], q[f, 17, t]
            first = gx == 0
            last = gx == n_gx - 1
            q[f, 0, t] = jnp.where(row < 4, jnp.where(first, z0, lower), sub(z14, 4))
            q[f, 1, t] = jnp.where(row < 4, jnp.where(first, z0, sub(lower, 4)), sub(z15, 4))
            q[f, 18, t] = jnp.where(row < 4, sub(z0, 4), jnp.where(last, z15, sub(upper, 4)))
            q[f, 19, t] = jnp.where(row < 4, sub(z1, 4), jnp.where(last, z15, upper))
        return 0

    lax.fori_loop(0, F, fill_z, 0)

    conduct(1)
    conduct(18)

    def along_z(t, _):
        for i in range(17):
            wz[i] = 0.125 * (q[2, i + 1, t] + q[2, i + 2, t])
            cz[i] = cond[i + 1, t] + cond[i + 2, t]

        def field(f, _):
            spread = diff_ref[f]
            here = q[f, 1, t]
            d_low = here - q[f, 0, t]
            after = q[f, 2, t]
            d = after - here
            left = here + 0.5 * minmod(d_low, d)
            before = None
            for i in range(17):
                here = after
                after = q[f, i + 3, t]
                d_next = after - here
                half = 0.5 * minmod(d, d_next)
                net = face(wz[i], cz[i], spread, d, left, here - half)
                left = here + half
                d = d_next
                if i > 0:
                    total = acc[f, i - 1, t - 1] + (net - before)
                    start = pl.multiple_of((i - 1) * PLANE + (t - 1) * 128, 128)
                    out_ref[f, :, pl.ds(start, 128)] = total[:4]
                    out_ref[f, :, pl.ds(start + 16 * PLANE, 128)] = total[4:]
                before = net
            return 0

        lax.fori_loop(0, F, field, 0)
        return 0

    lax.fori_loop(1, TILES + 1, along_z, 0)

    def finish(k, _):
        move(0, k).wait_send()
        move(1, k).wait_send()

        @pl.when(gy < n_gy - 1)
        def _():
            y_copy(0, k).wait_send()

        @pl.when(gy > 0)
        def _():
            y_copy(1, k).wait_send()

        return 0

    lax.fori_loop(0, CHUNKS, finish, 0)

    @pl.when(gx < n_gx - 1)
    def _():
        z_copy(0).wait_send()

    @pl.when(gx > 0)
    def _():
        z_copy(1).wait_send()


def solution(mesh):
    n_gx, n_gy = mesh.shape["gx"], mesh.shape["gy"]

    def local(old_state, old_owner, old_slot, diffusivity):
        def body(*refs):
            kernel(n_gx, n_gy, *refs)

        vmem = pltpu.VMEM
        dma = pltpu.SemaphoreType.DMA
        cells = old_state.shape[2]
        result = pl.pallas_call(
            body,
            out_shape=jax.ShapeDtypeStruct((F, CAP, cells), jnp.float32),
            in_specs=[
                pl.BlockSpec(memory_space=pltpu.SMEM),
                pl.BlockSpec(memory_space=pltpu.SMEM),
                pl.BlockSpec(memory_space=pl.ANY),
            ],
            out_specs=pl.BlockSpec(memory_space=pltpu.VMEM),
            scratch_shapes=[
                vmem((F, 8, cells), jnp.float32),
                vmem((2, CHUNKS, F, TILES, 8, 128), jnp.float32),
                vmem((2, CHUNKS, F, TILES, 8, 128), jnp.float32),
                vmem((F, 20, TILES + 2, 8, 128), jnp.float32),
                vmem((20, TILES + 2, 8, 128), jnp.float32),
                vmem((F, 16, TILES, 8, 128), jnp.float32),
                vmem((17, 8, 128), jnp.float32),
                vmem((17, 8, 128), jnp.float32),
                vmem((TILES + 2, 8, 128), jnp.float32),
                vmem((TILES + 2, 8, 128), jnp.float32),
                vmem((TILES + 2, 8, 128), jnp.float32),
                vmem((TILES + 2, 8, 128), jnp.float32),
                vmem((2, F, TILES, 8, 128), jnp.float32),
                vmem((2, F, TILES, 8, 128), jnp.float32),
                vmem((2, CHUNKS, F, 8, 128), jnp.float32),
                vmem((2, CHUNKS, F, 8, 128), jnp.float32),
                dma((CHUNKS, 4)),
                dma((2, CHUNKS)),
                dma((2, CHUNKS)),
                dma((2,)),
                dma((2,)),
                dma((2, CHUNKS)),
                dma((2, CHUNKS)),
            ],
            compiler_params=pltpu.CompilerParams(
                collective_id=0, has_side_effects=True, vmem_limit_bytes=56 * 2**20
            ),
        )(old_owner, diffusivity, jnp.transpose(old_state, (1, 0, 2)))
        return jnp.transpose(result, (1, 0, 2))

    placed = (P(("gx", "gy"), None, None), P(), P(), P())
    return jax.shard_map(
        local, mesh=mesh, in_specs=placed, out_specs=P(("gx", "gy"), None, None), check_vma=False
    )
```

```python
import jax
import jax.numpy as jnp
from jax import lax
from jax.experimental import pallas as pl
from jax.experimental.pallas import tpu as pltpu
from jax.sharding import PartitionSpec as P

F = 6
CAP = 4
CHUNKS = 8
TILES = 8
PLANE = 1024
MESH = pl.DeviceIdType.MESH


def kernel(
    n_gx, n_gy, owner_ref, diff_ref, state_ref, out_ref,
    held, send, recv, q, cond, acc, wz, cz, wy, cy, wx, cx,
    dy, dx, hy, hx, ny, nx, zsend, zrecv, ysend, yrecv,
    in_sem, move_send, move_recv, z_send, z_recv, y_send, y_recv,
):
    gx = lax.axis_index("gx")
    gy = lax.axis_index("gy")
    count = n_gx * n_gy
    me = gx * n_gy + gy
    above = lax.rem(me + 1, count)
    below = lax.rem(me + count - 1, count)
    ring = ((above // n_gy, lax.rem(above, n_gy)), (below // n_gy, lax.rem(below, n_gy)))

    def in_copy(k, part):
        cells = pl.ds(pl.multiple_of((k + 8 * part) * PLANE, PLANE), PLANE)
        return pltpu.make_async_copy(
            state_ref.at[:, :, cells], held.at[:, :, cells], in_sem.at[k, part]
        )

    def start_in(k, _):
        for part in range(4):
            in_copy(k, part).start()
        return 0

    lax.fori_loop(0, CHUNKS, start_in, 0)

    barrier = pltpu.get_barrier_semaphore()
    for target in ring:
        pl.semaphore_signal(barrier, inc=1, device_id=target, device_id_type=MESH)

    @pl.when(gx > 0)
    def _():
        pl.semaphore_signal(barrier, inc=1, device_id=(gx - 1, gy), device_id_type=MESH)

    @pl.when(gx < n_gx - 1)
    def _():
        pl.semaphore_signal(barrier, inc=1, device_id=(gx + 1, gy), device_id_type=MESH)

    pl.semaphore_wait(
        barrier, 2 + (gx > 0).astype(jnp.int32) + (gx < n_gx - 1).astype(jnp.int32)
    )

    row = lax.broadcasted_iota(jnp.int32, (8, 128), 0)
    lane = lax.broadcasted_iota(jnp.int32, (8, 128), 1)
    box = row % 4
    col = lane % 32

    def sub(values, shift):
        return pltpu.roll(values, shift % 8, 0)

    def turn(values, shift):
        return pltpu.roll(values, shift % 128, 1)

    def each_field(work):
        def group(g, _):
            for f in range(F // 2):
                work(g * (F // 2) + f)
            return 0

        lax.fori_loop(0, 2, group, 0)

    def tile_of(f, k, part, t):
        start = pl.multiple_of((k + 8 * part) * PLANE + t * 128, 128)
        return held[f, :, pl.ds(start, 128)]

    def move(way, k):
        return pltpu.make_async_remote_copy(
            src_ref=send.at[way, k],
            dst_ref=recv.at[way, k],
            send_sem=move_send.at[way, k],
            recv_sem=move_recv.at[way, k],
            device_id=ring[way],
            device_id_type=MESH,
        )

    def pack(k, _):
        for part in range(4):
            in_copy(k, part).wait()

        def field(f):
            for t in range(TILES):
                a, b, c, d = (tile_of(f, k, part, t) for part in range(4))
                a2, c6 = sub(a, 2), sub(c, 6)
                up = jnp.where(
                    row < 4, jnp.where(row < 2, a2, sub(b, 4)), jnp.where(row < 6, c6, d)
                )
                down = jnp.where(
                    row < 4, jnp.where(row < 2, b, a2), jnp.where(row < 6, sub(d, 4), c6)
                )
                send[0, k, f, t] = up
                send[1, k, f, t] = down

        each_field(field)
        move(0, k).start()
        move(1, k).start()
        return 0

    lax.fori_loop(0, CHUNKS, pack, 0)

    owners = jnp.zeros((8, 128), jnp.int32)
    for c in range(CAP):
        owners = jnp.where(box == c, owner_ref[me * CAP + c], owners)
    kept = owners == me

    def y_copy(way, k):
        return pltpu.make_async_remote_copy(
            src_ref=ysend.at[way, k],
            dst_ref=yrecv.at[way, k],
            send_sem=y_send.at[way, k],
            recv_sem=y_recv.at[way, k],
            device_id=(gx, gy + 1) if way == 0 else (gx, gy - 1),
            device_id_type=MESH,
        )

    def z_copy(way):
        return pltpu.make_async_remote_copy(
            src_ref=zsend.at[way],
            dst_ref=zrecv.at[way],
            send_sem=z_send.at[way],
            recv_sem=z_recv.at[way],
            device_id=(gx + 1, gy) if way == 0 else (gx - 1, gy),
            device_id_type=MESH,
        )

    def gather(k):
        move(0, k).wait_recv()
        move(1, k).wait_recv()

        def field(f):
            for t in range(TILES):
                a, b, c, d = (tile_of(f, k, part, t) for part in range(4))
                up = recv[0, k, f, t]
                down = recv[1, k, f, t]
                first = jnp.where(
                    kept,
                    jnp.where(row < 4, sub(a, 6), sub(c, 2)),
                    jnp.where(box < 2, up, down),
                )
                second = jnp.where(
                    kept,
                    jnp.where(row < 4, sub(b, 6), sub(d, 2)),
                    jnp.where(box < 2, sub(up, 6), sub(down, 2)),
                )
                q[f, k + 2, t + 1] = first
                q[f, k + 10, t + 1] = second
                if t == 0:
                    ysend[1, k, f] = jnp.where(lane < 64, first, turn(second, 64))
                if t == TILES - 1:
                    ysend[0, k, f] = jnp.where(lane < 64, turn(second, 64), first)

        each_field(field)

        @pl.when(gy < n_gy - 1)
        def _():
            y_copy(0, k).start()

        @pl.when(gy > 0)
        def _():
            y_copy(1, k).start()

    def fill_y(k):
        @pl.when(gy > 0)
        def _():
            y_copy(0, k).wait_recv()

        @pl.when(gy < n_gy - 1)
        def _():
            y_copy(1, k).wait_recv()

        def field(f):
            lower = yrecv[0, k, f]
            upper = yrecv[1, k, f]
            for plane, low, high in (
                (k + 2, lower, upper), (k + 10, turn(lower, 64), turn(upper, 64))
            ):
                bottom = q[f, plane, 1]
                top = q[f, plane, TILES]
                q[f, plane, 0] = jnp.where(
                    gy == 0, jnp.where(lane < 96, turn(bottom, 64), turn(bottom, 96)), low
                )
                q[f, plane, TILES + 1] = jnp.where(
                    gy == n_gy - 1, jnp.where(lane < 32, turn(top, 32), turn(top, 64)), high
                )

        each_field(field)

    def conduct(z):
        for t in range(TILES + 2):
            cond[z, t] = 0.5 * jnp.exp(0.5 * jnp.tanh(q[5, z, t]))

    def minmod(a, b):
        return jnp.maximum(jnp.minimum(a, b), jnp.minimum(jnp.maximum(a, b), 0.0))

    def face(w, c, spread, d, left, right):
        return spread * c * d - w * jnp.where(w > 0.0, left, right)

    edge_low = (box == 0) & (col == 0)
    edge_high = (box == 3) & (col == 31)

    def x_next(values):
        return jnp.where(col == 31, sub(turn(values, 31), -1), turn(values, -1))

    def x_back(values):
        return jnp.where(col == 0, sub(turn(values, -31), 1), turn(values, 1))

    def y_next(values, later):
        return turn(jnp.where(lane < 32, later, values), -32)

    def y_back(values, earlier):
        return turn(jnp.where(lane >= 96, earlier, values), 32)

    def send_z():
        def pack_z(f, _):
            for t in range(1, TILES + 1):
                zsend[1, f, t - 1] = jnp.where(row < 4, q[f, 2, t], sub(q[f, 3, t], 4))
                zsend[0, f, t - 1] = jnp.where(row < 4, sub(q[f, 16, t], 4), q[f, 17, t])
            return 0

        lax.fori_loop(0, F, pack_z, 0)

        @pl.when(gx < n_gx - 1)
        def _():
            z_copy(0).start()

        @pl.when(gx > 0)
        def _():
            z_copy(1).start()

    def along_yx(z):
        conduct(z)
        for t in range(TILES + 1):
            u, c = q[1, z, t], cond[z, t]
            wy[t] = 0.125 * (u + y_next(u, q[1, z, t + 1]))
            cy[t] = c + y_next(c, cond[z, t + 1])
        for t in range(1, TILES + 1):
            u, c = q[0, z, t], cond[z, t]
            wx[t] = 0.125 * (u + jnp.where(edge_high, u, x_next(u)))
            cx[t] = c + jnp.where(edge_high, c, x_next(c))

        def differences(f):
            vals = [q[f, z, t] for t in range(TILES + 2)]
            for t in range(TILES + 2):
                dy[f, t] = y_next(vals[t], vals[min(t + 1, TILES + 1)]) - vals[t]
            for t in range(1, TILES + 1):
                dx[f, t] = jnp.where(edge_high, 0.0, x_next(vals[t]) - vals[t])

        def slopes(f):
            diffs = [dy[f, t] for t in range(TILES + 2)]
            for t in range(TILES + 2):
                hy[f, t] = 0.5 * minmod(y_back(diffs[t], diffs[max(t - 1, 0)]), diffs[t])
            for t in range(1, TILES + 1):
                d = dx[f, t]
                hx[f, t] = 0.5 * minmod(jnp.where(edge_low, 0.0, x_back(d)), d)

        def fluxes(f):
            spread = diff_ref[f]
            vals = [q[f, z, t] for t in range(TILES + 2)]
            halves = [hy[f, t] for t in range(TILES + 2)]
            rights = [v - h for v, h in zip(vals, halves)]
            for t in range(TILES + 1):
                ny[f, t] = face(
                    wy[t], cy[t], spread, dy[f, t], vals[t] + halves[t],
                    y_next(rights[t], rights[t + 1]),
                )
            for t in range(1, TILES + 1):
                v, half = vals[t], hx[f, t]
                right = jnp.where(edge_high, v, x_next(v - half))
                nx[f, t] = face(wx[t], cx[t], spread, dx[f, t], v + half, right)

        def sums(f):
            nets = [ny[f, t] for t in range(TILES + 1)]
            for t in range(1, TILES + 1):
                v, net = q[f, z, t], nx[f, t]
                total = v + (nets[t] - y_back(nets[t], nets[t - 1]))
                low = jnp.where(edge_low, -0.25 * q[0, z, t] * v, x_back(net))
                acc[f, z - 2, t - 1] = total + (net - low)

        each_field(differences)
        each_field(slopes)
        each_field(fluxes)
        each_field(sums)

    def update(k):
        fill_y(k)

        def plane(i, _):
            along_yx(k + 2 + 8 * i)
            return 0

        lax.fori_loop(0, 2, plane, 0)

    def step(k, _):
        @pl.when(k < CHUNKS)
        def _():
            gather(k)

        @pl.when(k == CHUNKS)
        def _():
            send_z()

        @pl.when(k > 0)
        def _():
            update(k - 1)

        return 0

    lax.fori_loop(0, CHUNKS + 1, step, 0)

    @pl.when(gx > 0)
    def _():
        z_copy(0).wait_recv()

    @pl.when(gx < n_gx - 1)
    def _():
        z_copy(1).wait_recv()

    def fill_z(f, _):
        for t in range(1, TILES + 1):
            lower = zrecv[0, f, t - 1]
            upper = zrecv[1, f, t - 1]
            z0, z1, z14, z15 = q[f, 2, t], q[f, 3, t], q[f, 16, t], q[f, 17, t]
            first = gx == 0
            last = gx == n_gx - 1
            q[f, 0, t] = jnp.where(row < 4, jnp.where(first, z0, lower), sub(z14, 4))
            q[f, 1, t] = jnp.where(row < 4, jnp.where(first, z0, sub(lower, 4)), sub(z15, 4))
            q[f, 18, t] = jnp.where(row < 4, sub(z0, 4), jnp.where(last, z15, sub(upper, 4)))
            q[f, 19, t] = jnp.where(row < 4, sub(z1, 4), jnp.where(last, z15, upper))
        return 0

    lax.fori_loop(0, F, fill_z, 0)

    conduct(1)
    conduct(18)

    def along_z(t, _):
        for i in range(17):
            wz[i] = 0.125 * (q[2, i + 1, t] + q[2, i + 2, t])
            cz[i] = cond[i + 1, t] + cond[i + 2, t]

        def field(f, _):
            spread = diff_ref[f]
            here = q[f, 1, t]
            d_low = here - q[f, 0, t]
            after = q[f, 2, t]
            d = after - here
            left = here + 0.5 * minmod(d_low, d)
            before = None
            for i in range(17):
                here = after
                after = q[f, i + 3, t]
                d_next = after - here
                half = 0.5 * minmod(d, d_next)
                net = face(wz[i], cz[i], spread, d, left, here - half)
                left = here + half
                d = d_next
                if i > 0:
                    total = acc[f, i - 1, t - 1] + (net - before)
                    start = pl.multiple_of((i - 1) * PLANE + (t - 1) * 128, 128)
                    out_ref[f, :, pl.ds(start, 128)] = total[:4]
                    out_ref[f, :, pl.ds(start + 16 * PLANE, 128)] = total[4:]
                before = net
            return 0

        lax.fori_loop(0, F, field, 0)
        return 0

    lax.fori_loop(1, TILES + 1, along_z, 0)

    def finish(k, _):
        move(0, k).wait_send()
        move(1, k).wait_send()

        @pl.when(gy < n_gy - 1)
        def _():
            y_copy(0, k).wait_send()

        @pl.when(gy > 0)
        def _():
            y_copy(1, k).wait_send()

        return 0

    lax.fori_loop(0, CHUNKS, finish, 0)

    @pl.when(gx < n_gx - 1)
    def _():
        z_copy(0).wait_send()

    @pl.when(gx > 0)
    def _():
        z_copy(1).wait_send()


def solution(mesh):
    n_gx, n_gy = mesh.shape["gx"], mesh.shape["gy"]

    def local(old_state, old_owner, old_slot, diffusivity):
        def body(*refs):
            kernel(n_gx, n_gy, *refs)

        vmem = pltpu.VMEM
        dma = pltpu.SemaphoreType.DMA
        cells = old_state.shape[2]
        result = pl.pallas_call(
            body,
            out_shape=jax.ShapeDtypeStruct((F, CAP, cells), jnp.float32),
            in_specs=[
                pl.BlockSpec(memory_space=pltpu.SMEM),
                pl.BlockSpec(memory_space=pltpu.SMEM),
                pl.BlockSpec(memory_space=pl.ANY),
            ],
            out_specs=pl.BlockSpec(memory_space=pltpu.VMEM),
            scratch_shapes=[
                vmem((F, 8, cells), jnp.float32),
                vmem((2, CHUNKS, F, TILES, 8, 128), jnp.float32),
                vmem((2, CHUNKS, F, TILES, 8, 128), jnp.float32),
                vmem((F, 20, TILES + 2, 8, 128), jnp.float32),
                vmem((20, TILES + 2, 8, 128), jnp.float32),
                vmem((F, 16, TILES, 8, 128), jnp.float32),
                vmem((17, 8, 128), jnp.float32),
                vmem((17, 8, 128), jnp.float32),
                vmem((TILES + 2, 8, 128), jnp.float32),
                vmem((TILES + 2, 8, 128), jnp.float32),
                vmem((TILES + 2, 8, 128), jnp.float32),
                vmem((TILES + 2, 8, 128), jnp.float32),
                *[vmem((F, TILES + 2, 8, 128), jnp.float32) for _ in range(6)],
                vmem((2, F, TILES, 8, 128), jnp.float32),
                vmem((2, F, TILES, 8, 128), jnp.float32),
                vmem((2, CHUNKS, F, 8, 128), jnp.float32),
                vmem((2, CHUNKS, F, 8, 128), jnp.float32),
                dma((CHUNKS, 4)),
                dma((2, CHUNKS)),
                dma((2, CHUNKS)),
                dma((2,)),
                dma((2,)),
                dma((2, CHUNKS)),
                dma((2, CHUNKS)),
            ],
            compiler_params=pltpu.CompilerParams(
                collective_id=0, has_side_effects=True, vmem_limit_bytes=56 * 2**20
            ),
        )(old_owner, diffusivity, jnp.transpose(old_state, (1, 0, 2)))
        return jnp.transpose(result, (1, 0, 2))

    placed = (P(("gx", "gy"), None, None), P(), P(), P())
    return jax.shard_map(
        local, mesh=mesh, in_specs=placed, out_specs=P(("gx", "gy"), None, None), check_vma=False
    )
```

```python
import jax
import jax.numpy as jnp
from jax import lax
from jax.experimental import pallas as pl
from jax.experimental.pallas import tpu as pltpu
from jax.sharding import PartitionSpec as P

F = 6
CAP = 4
AHEAD = 2
CHUNKS = 8
TILES = 8
PLANE = 1024
MESH = pl.DeviceIdType.MESH


def kernel(
    n_gx, n_gy, owner_ref, diff_ref, state_ref, out_ref,
    held, send, recv, q, cond, acc, wz, cz, wy, cy, wx, cx,
    dy, dx, hy, hx, ny, nx, zsend, zrecv, ysend, yrecv,
    in_sem, move_send, move_recv, z_send, z_recv, y_send, y_recv,
):
    gx = lax.axis_index("gx")
    gy = lax.axis_index("gy")
    count = n_gx * n_gy
    me = gx * n_gy + gy
    above = lax.rem(me + 1, count)
    below = lax.rem(me + count - 1, count)
    ring = ((above // n_gy, lax.rem(above, n_gy)), (below // n_gy, lax.rem(below, n_gy)))

    def in_copy(k, part):
        cells = pl.ds(pl.multiple_of((k + 8 * part) * PLANE, PLANE), PLANE)
        return pltpu.make_async_copy(
            state_ref.at[:, :, cells], held.at[:, :, cells], in_sem.at[k, part]
        )

    def start_in(k, _):
        for part in range(4):
            in_copy(k, part).start()
        return 0

    lax.fori_loop(0, CHUNKS, start_in, 0)

    barrier = pltpu.get_barrier_semaphore()
    for target in ring:
        pl.semaphore_signal(barrier, inc=1, device_id=target, device_id_type=MESH)

    @pl.when(gx > 0)
    def _():
        pl.semaphore_signal(barrier, inc=1, device_id=(gx - 1, gy), device_id_type=MESH)

    @pl.when(gx < n_gx - 1)
    def _():
        pl.semaphore_signal(barrier, inc=1, device_id=(gx + 1, gy), device_id_type=MESH)

    pl.semaphore_wait(
        barrier, 2 + (gx > 0).astype(jnp.int32) + (gx < n_gx - 1).astype(jnp.int32)
    )

    row = lax.broadcasted_iota(jnp.int32, (8, 128), 0)
    lane = lax.broadcasted_iota(jnp.int32, (8, 128), 1)
    box = row % 4
    col = lane % 32

    def sub(values, shift):
        return pltpu.roll(values, shift % 8, 0)

    def turn(values, shift):
        return pltpu.roll(values, shift % 128, 1)

    def each_field(work):
        def group(g, _):
            for f in range(F // 2):
                work(g * (F // 2) + f)
            return 0

        lax.fori_loop(0, 2, group, 0)

    def tile_of(f, k, part, t):
        start = pl.multiple_of((k + 8 * part) * PLANE + t * 128, 128)
        return held[f, :, pl.ds(start, 128)]

    def move(way, k):
        return pltpu.make_async_remote_copy(
            src_ref=send.at[way, k],
            dst_ref=recv.at[way, k],
            send_sem=move_send.at[way, k],
            recv_sem=move_recv.at[way, k],
            device_id=ring[way],
            device_id_type=MESH,
        )

    def start_move(k):
        move(0, k).start()
        move(1, k).start()

    def pack(k, _):
        for part in range(4):
            in_copy(k, part).wait()

        def field(f):
            for t in range(TILES):
                a, b, c, d = (tile_of(f, k, part, t) for part in range(4))
                a2, c6 = sub(a, 2), sub(c, 6)
                up = jnp.where(
                    row < 4, jnp.where(row < 2, a2, sub(b, 4)), jnp.where(row < 6, c6, d)
                )
                down = jnp.where(
                    row < 4, jnp.where(row < 2, b, a2), jnp.where(row < 6, sub(d, 4), c6)
                )
                send[0, k, f, t] = up
                send[1, k, f, t] = down

        each_field(field)
        @pl.when(k < AHEAD)
        def _():
            start_move(k)

        return 0

    lax.fori_loop(0, CHUNKS, pack, 0)

    owners = jnp.zeros((8, 128), jnp.int32)
    for c in range(CAP):
        owners = jnp.where(box == c, owner_ref[me * CAP + c], owners)
    kept = owners == me

    def y_copy(way, k):
        return pltpu.make_async_remote_copy(
            src_ref=ysend.at[way, k],
            dst_ref=yrecv.at[way, k],
            send_sem=y_send.at[way, k],
            recv_sem=y_recv.at[way, k],
            device_id=(gx, gy + 1) if way == 0 else (gx, gy - 1),
            device_id_type=MESH,
        )

    def z_copy(way):
        return pltpu.make_async_remote_copy(
            src_ref=zsend.at[way],
            dst_ref=zrecv.at[way],
            send_sem=z_send.at[way],
            recv_sem=z_recv.at[way],
            device_id=(gx + 1, gy) if way == 0 else (gx - 1, gy),
            device_id_type=MESH,
        )

    def gather(k):
        move(0, k).wait_recv()
        move(1, k).wait_recv()

        @pl.when(k < CHUNKS - AHEAD)
        def _():
            start_move(k + AHEAD)

        def field(f):
            for t in range(TILES):
                a, b, c, d = (tile_of(f, k, part, t) for part in range(4))
                up = recv[0, k, f, t]
                down = recv[1, k, f, t]
                first = jnp.where(
                    kept,
                    jnp.where(row < 4, sub(a, 6), sub(c, 2)),
                    jnp.where(box < 2, up, down),
                )
                second = jnp.where(
                    kept,
                    jnp.where(row < 4, sub(b, 6), sub(d, 2)),
                    jnp.where(box < 2, sub(up, 6), sub(down, 2)),
                )
                q[f, k + 2, t + 1] = first
                q[f, k + 10, t + 1] = second
                if t == 0:
                    ysend[1, k, f] = jnp.where(lane < 64, first, turn(second, 64))
                if t == TILES - 1:
                    ysend[0, k, f] = jnp.where(lane < 64, turn(second, 64), first)

        each_field(field)

        @pl.when(gy < n_gy - 1)
        def _():
            y_copy(0, k).start()

        @pl.when(gy > 0)
        def _():
            y_copy(1, k).start()

    def fill_y(k):
        @pl.when(gy > 0)
        def _():
            y_copy(0, k).wait_recv()

        @pl.when(gy < n_gy - 1)
        def _():
            y_copy(1, k).wait_recv()

        def field(f):
            lower = yrecv[0, k, f]
            upper = yrecv[1, k, f]
            for plane, low, high in (
                (k + 2, lower, upper), (k + 10, turn(lower, 64), turn(upper, 64))
            ):
                bottom = q[f, plane, 1]
                top = q[f, plane, TILES]
                q[f, plane, 0] = jnp.where(
                    gy == 0, jnp.where(lane < 96, turn(bottom, 64), turn(bottom, 96)), low
                )
                q[f, plane, TILES + 1] = jnp.where(
                    gy == n_gy - 1, jnp.where(lane < 32, turn(top, 32), turn(top, 64)), high
                )

        each_field(field)

    def conduct(z):
        for t in range(TILES + 2):
            cond[z, t] = 0.5 * jnp.exp(0.5 * jnp.tanh(q[5, z, t]))

    def minmod(a, b):
        return jnp.maximum(jnp.minimum(a, b), jnp.minimum(jnp.maximum(a, b), 0.0))

    def face(w, c, spread, d, left, right):
        return spread * c * d - w * jnp.where(w > 0.0, left, right)

    edge_low = (box == 0) & (col == 0)
    edge_high = (box == 3) & (col == 31)

    def x_next(values):
        return jnp.where(col == 31, sub(turn(values, 31), -1), turn(values, -1))

    def x_back(values):
        return jnp.where(col == 0, sub(turn(values, -31), 1), turn(values, 1))

    def y_next(values, later):
        return turn(jnp.where(lane < 32, later, values), -32)

    def y_back(values, earlier):
        return turn(jnp.where(lane >= 96, earlier, values), 32)

    def send_z():
        def pack_z(f, _):
            for t in range(1, TILES + 1):
                zsend[1, f, t - 1] = jnp.where(row < 4, q[f, 2, t], sub(q[f, 3, t], 4))
                zsend[0, f, t - 1] = jnp.where(row < 4, sub(q[f, 16, t], 4), q[f, 17, t])
            return 0

        lax.fori_loop(0, F, pack_z, 0)

        @pl.when(gx < n_gx - 1)
        def _():
            z_copy(0).start()

        @pl.when(gx > 0)
        def _():
            z_copy(1).start()

    def along_yx(z):
        conduct(z)
        for t in range(TILES + 1):
            u, c = q[1, z, t], cond[z, t]
            wy[t] = 0.125 * (u + y_next(u, q[1, z, t + 1]))
            cy[t] = c + y_next(c, cond[z, t + 1])
        for t in range(1, TILES + 1):
            u, c = q[0, z, t], cond[z, t]
            wx[t] = 0.125 * (u + jnp.where(edge_high, u, x_next(u)))
            cx[t] = c + jnp.where(edge_high, c, x_next(c))

        def differences(f):
            vals = [q[f, z, t] for t in range(TILES + 2)]
            for t in range(TILES + 2):
                dy[f, t] = y_next(vals[t], vals[min(t + 1, TILES + 1)]) - vals[t]
            for t in range(1, TILES + 1):
                dx[f, t] = jnp.where(edge_high, 0.0, x_next(vals[t]) - vals[t])

        def slopes(f):
            diffs = [dy[f, t] for t in range(TILES + 2)]
            for t in range(TILES + 2):
                hy[f, t] = 0.5 * minmod(y_back(diffs[t], diffs[max(t - 1, 0)]), diffs[t])
            for t in range(1, TILES + 1):
                d = dx[f, t]
                hx[f, t] = 0.5 * minmod(jnp.where(edge_low, 0.0, x_back(d)), d)

        def fluxes(f):
            spread = diff_ref[f]
            vals = [q[f, z, t] for t in range(TILES + 2)]
            halves = [hy[f, t] for t in range(TILES + 2)]
            rights = [v - h for v, h in zip(vals, halves)]
            for t in range(TILES + 1):
                ny[f, t] = face(
                    wy[t], cy[t], spread, dy[f, t], vals[t] + halves[t],
                    y_next(rights[t], rights[t + 1]),
                )
            for t in range(1, TILES + 1):
                v, half = vals[t], hx[f, t]
                right = jnp.where(edge_high, v, x_next(v - half))
                nx[f, t] = face(wx[t], cx[t], spread, dx[f, t], v + half, right)

        def sums(f):
            nets = [ny[f, t] for t in range(TILES + 1)]
            for t in range(1, TILES + 1):
                v, net = q[f, z, t], nx[f, t]
                total = v + (nets[t] - y_back(nets[t], nets[t - 1]))
                low = jnp.where(edge_low, -0.25 * q[0, z, t] * v, x_back(net))
                acc[f, z - 2, t - 1] = total + (net - low)

        each_field(differences)
        each_field(slopes)
        each_field(fluxes)
        each_field(sums)

    def update(k):
        fill_y(k)

        def plane(i, _):
            along_yx(k + 2 + 8 * i)
            return 0

        lax.fori_loop(0, 2, plane, 0)

    def step(k, _):
        @pl.when(k < CHUNKS)
        def _():
            gather(k)

        @pl.when(k == CHUNKS)
        def _():
            send_z()

        @pl.when(k >= AHEAD)
        def _():
            update(k - AHEAD)

        return 0

    lax.fori_loop(0, CHUNKS + AHEAD, step, 0)

    @pl.when(gx > 0)
    def _():
        z_copy(0).wait_recv()

    @pl.when(gx < n_gx - 1)
    def _():
        z_copy(1).wait_recv()

    def fill_z(f, _):
        for t in range(1, TILES + 1):
            lower = zrecv[0, f, t - 1]
            upper = zrecv[1, f, t - 1]
            z0, z1, z14, z15 = q[f, 2, t], q[f, 3, t], q[f, 16, t], q[f, 17, t]
            first = gx == 0
            last = gx == n_gx - 1
            q[f, 0, t] = jnp.where(row < 4, jnp.where(first, z0, lower), sub(z14, 4))
            q[f, 1, t] = jnp.where(row < 4, jnp.where(first, z0, sub(lower, 4)), sub(z15, 4))
            q[f, 18, t] = jnp.where(row < 4, sub(z0, 4), jnp.where(last, z15, sub(upper, 4)))
            q[f, 19, t] = jnp.where(row < 4, sub(z1, 4), jnp.where(last, z15, upper))
        return 0

    lax.fori_loop(0, F, fill_z, 0)

    conduct(1)
    conduct(18)

    def along_z(t, _):
        for i in range(17):
            wz[i] = 0.125 * (q[2, i + 1, t] + q[2, i + 2, t])
            cz[i] = cond[i + 1, t] + cond[i + 2, t]

        def field(f, _):
            spread = diff_ref[f]
            here = q[f, 1, t]
            d_low = here - q[f, 0, t]
            after = q[f, 2, t]
            d = after - here
            left = here + 0.5 * minmod(d_low, d)
            before = None
            for i in range(17):
                here = after
                after = q[f, i + 3, t]
                d_next = after - here
                half = 0.5 * minmod(d, d_next)
                net = face(wz[i], cz[i], spread, d, left, here - half)
                left = here + half
                d = d_next
                if i > 0:
                    total = acc[f, i - 1, t - 1] + (net - before)
                    start = pl.multiple_of((i - 1) * PLANE + (t - 1) * 128, 128)
                    out_ref[f, :, pl.ds(start, 128)] = total[:4]
                    out_ref[f, :, pl.ds(start + 16 * PLANE, 128)] = total[4:]
                before = net
            return 0

        lax.fori_loop(0, F, field, 0)
        return 0

    lax.fori_loop(1, TILES + 1, along_z, 0)

    def finish(k, _):
        move(0, k).wait_send()
        move(1, k).wait_send()

        @pl.when(gy < n_gy - 1)
        def _():
            y_copy(0, k).wait_send()

        @pl.when(gy > 0)
        def _():
            y_copy(1, k).wait_send()

        return 0

    lax.fori_loop(0, CHUNKS, finish, 0)

    @pl.when(gx < n_gx - 1)
    def _():
        z_copy(0).wait_send()

    @pl.when(gx > 0)
    def _():
        z_copy(1).wait_send()


def solution(mesh):
    n_gx, n_gy = mesh.shape["gx"], mesh.shape["gy"]

    def local(old_state, old_owner, old_slot, diffusivity):
        def body(*refs):
            kernel(n_gx, n_gy, *refs)

        vmem = pltpu.VMEM
        dma = pltpu.SemaphoreType.DMA
        cells = old_state.shape[2]
        result = pl.pallas_call(
            body,
            out_shape=jax.ShapeDtypeStruct((F, CAP, cells), jnp.float32),
            in_specs=[
                pl.BlockSpec(memory_space=pltpu.SMEM),
                pl.BlockSpec(memory_space=pltpu.SMEM),
                pl.BlockSpec(memory_space=pl.ANY),
            ],
            out_specs=pl.BlockSpec(memory_space=pltpu.VMEM),
            scratch_shapes=[
                vmem((F, 8, cells), jnp.float32),
                vmem((2, CHUNKS, F, TILES, 8, 128), jnp.float32),
                vmem((2, CHUNKS, F, TILES, 8, 128), jnp.float32),
                vmem((F, 20, TILES + 2, 8, 128), jnp.float32),
                vmem((20, TILES + 2, 8, 128), jnp.float32),
                vmem((F, 16, TILES, 8, 128), jnp.float32),
                vmem((17, 8, 128), jnp.float32),
                vmem((17, 8, 128), jnp.float32),
                vmem((TILES + 2, 8, 128), jnp.float32),
                vmem((TILES + 2, 8, 128), jnp.float32),
                vmem((TILES + 2, 8, 128), jnp.float32),
                vmem((TILES + 2, 8, 128), jnp.float32),
                *[vmem((F, TILES + 2, 8, 128), jnp.float32) for _ in range(6)],
                vmem((2, F, TILES, 8, 128), jnp.float32),
                vmem((2, F, TILES, 8, 128), jnp.float32),
                vmem((2, CHUNKS, F, 8, 128), jnp.float32),
                vmem((2, CHUNKS, F, 8, 128), jnp.float32),
                dma((CHUNKS, 4)),
                dma((2, CHUNKS)),
                dma((2, CHUNKS)),
                dma((2,)),
                dma((2,)),
                dma((2, CHUNKS)),
                dma((2, CHUNKS)),
            ],
            compiler_params=pltpu.CompilerParams(
                collective_id=0, has_side_effects=True, vmem_limit_bytes=56 * 2**20
            ),
        )(old_owner, diffusivity, jnp.transpose(old_state, (1, 0, 2)))
        return jnp.transpose(result, (1, 0, 2))

    placed = (P(("gx", "gy"), None, None), P(), P(), P())
    return jax.shard_map(
        local, mesh=mesh, in_specs=placed, out_specs=P(("gx", "gy"), None, None), check_vma=False
    )
```

```python
import jax
import jax.numpy as jnp
from jax import lax
from jax.experimental import pallas as pl
from jax.experimental.pallas import tpu as pltpu
from jax.sharding import PartitionSpec as P

F = 6
CAP = 4
AHEAD = 2
CHUNKS = 8
TILES = 8
PLANE = 1024
MESH = pl.DeviceIdType.MESH


def kernel(
    n_gx, n_gy, owner_ref, diff_ref, state_ref, out_ref,
    held, send, recv, q, cond, acc, wz, cz, wy, cy, wx, cx,
    dy, dx, hy, hx, ny, nx, zsend, zrecv, ysend, yrecv,
    in_sem, move_send, move_recv, z_send, z_recv, y_send, y_recv,
):
    gx = lax.axis_index("gx")
    gy = lax.axis_index("gy")
    count = n_gx * n_gy
    me = gx * n_gy + gy
    above = lax.rem(me + 1, count)
    below = lax.rem(me + count - 1, count)
    ring = ((above // n_gy, lax.rem(above, n_gy)), (below // n_gy, lax.rem(below, n_gy)))

    def in_copy(k, part):
        cells = pl.ds(pl.multiple_of((k + 8 * part) * PLANE, PLANE), PLANE)
        return pltpu.make_async_copy(
            state_ref.at[:, :, cells], held.at[:, :, cells], in_sem.at[k, part]
        )

    def start_in(k, _):
        for part in range(4):
            in_copy(k, part).start()
        return 0

    lax.fori_loop(0, CHUNKS, start_in, 0)

    barrier = pltpu.get_barrier_semaphore()
    for target in ring:
        pl.semaphore_signal(barrier, inc=1, device_id=target, device_id_type=MESH)

    @pl.when(gx > 0)
    def _():
        pl.semaphore_signal(barrier, inc=1, device_id=(gx - 1, gy), device_id_type=MESH)

    @pl.when(gx < n_gx - 1)
    def _():
        pl.semaphore_signal(barrier, inc=1, device_id=(gx + 1, gy), device_id_type=MESH)

    pl.semaphore_wait(
        barrier, 2 + (gx > 0).astype(jnp.int32) + (gx < n_gx - 1).astype(jnp.int32)
    )

    row = lax.broadcasted_iota(jnp.int32, (8, 128), 0)
    lane = lax.broadcasted_iota(jnp.int32, (8, 128), 1)
    box = row % 4
    col = lane % 32

    def sub(values, shift):
        return pltpu.roll(values, shift % 8, 0)

    def turn(values, shift):
        return pltpu.roll(values, shift % 128, 1)

    def each_field(work):
        def group(g, _):
            for f in range(F // 2):
                work(g * (F // 2) + f)
            return 0

        lax.fori_loop(0, 2, group, 0)

    def tile_of(f, k, part, t):
        start = pl.multiple_of((k + 8 * part) * PLANE + t * 128, 128)
        return held[f, :, pl.ds(start, 128)]

    def move(way, k):
        return pltpu.make_async_remote_copy(
            src_ref=send.at[way, k],
            dst_ref=recv.at[way, k],
            send_sem=move_send.at[way, k],
            recv_sem=move_recv.at[way, k],
            device_id=ring[way],
            device_id_type=MESH,
        )

    def start_move(k):
        move(0, k).start()
        move(1, k).start()

    def pack(k, _):
        for part in range(4):
            in_copy(k, part).wait()

        def field(f):
            for t in range(TILES):
                a, b, c, d = (tile_of(f, k, part, t) for part in range(4))
                a2, c6 = sub(a, 2), sub(c, 6)
                up = jnp.where(
                    row < 4, jnp.where(row < 2, a2, sub(b, 4)), jnp.where(row < 6, c6, d)
                )
                down = jnp.where(
                    row < 4, jnp.where(row < 2, b, a2), jnp.where(row < 6, sub(d, 4), c6)
                )
                send[0, k, f, t] = up
                send[1, k, f, t] = down

        each_field(field)
        @pl.when(k < AHEAD)
        def _():
            start_move(k)

        return 0

    lax.fori_loop(0, CHUNKS, pack, 0)

    owners = jnp.zeros((8, 128), jnp.int32)
    for c in range(CAP):
        owners = jnp.where(box == c, owner_ref[me * CAP + c], owners)
    kept = owners == me

    def y_copy(way, k):
        return pltpu.make_async_remote_copy(
            src_ref=ysend.at[way, k],
            dst_ref=yrecv.at[way, k],
            send_sem=y_send.at[way, k],
            recv_sem=y_recv.at[way, k],
            device_id=(gx, gy + 1) if way == 0 else (gx, gy - 1),
            device_id_type=MESH,
        )

    def z_copy(way):
        return pltpu.make_async_remote_copy(
            src_ref=zsend.at[way],
            dst_ref=zrecv.at[way],
            send_sem=z_send.at[way],
            recv_sem=z_recv.at[way],
            device_id=(gx + 1, gy) if way == 0 else (gx - 1, gy),
            device_id_type=MESH,
        )

    def gather(k):
        move(0, k).wait_recv()
        move(1, k).wait_recv()

        @pl.when(k < CHUNKS - AHEAD)
        def _():
            start_move(k + AHEAD)

        def field(f):
            for t in range(TILES):
                a, b, c, d = (tile_of(f, k, part, t) for part in range(4))
                up = recv[0, k, f, t]
                down = recv[1, k, f, t]
                first = jnp.where(
                    kept,
                    jnp.where(row < 4, sub(a, 6), sub(c, 2)),
                    jnp.where(box < 2, up, down),
                )
                second = jnp.where(
                    kept,
                    jnp.where(row < 4, sub(b, 6), sub(d, 2)),
                    jnp.where(box < 2, sub(up, 6), sub(down, 2)),
                )
                q[f, k + 2, t + 1] = first
                q[f, k + 10, t + 1] = second
                if t == 0:
                    ysend[1, k, f] = jnp.where(lane < 64, first, turn(second, 64))
                if t == TILES - 1:
                    ysend[0, k, f] = jnp.where(lane < 64, turn(second, 64), first)

        each_field(field)

        @pl.when(gy < n_gy - 1)
        def _():
            y_copy(0, k).start()

        @pl.when(gy > 0)
        def _():
            y_copy(1, k).start()

    def fill_y(k):
        @pl.when(gy > 0)
        def _():
            y_copy(0, k).wait_recv()

        @pl.when(gy < n_gy - 1)
        def _():
            y_copy(1, k).wait_recv()

        def field(f):
            lower = yrecv[0, k, f]
            upper = yrecv[1, k, f]
            for plane, low, high in (
                (k + 2, lower, upper), (k + 10, turn(lower, 64), turn(upper, 64))
            ):
                bottom = q[f, plane, 1]
                top = q[f, plane, TILES]
                q[f, plane, 0] = jnp.where(
                    gy == 0, jnp.where(lane < 96, turn(bottom, 64), turn(bottom, 96)), low
                )
                q[f, plane, TILES + 1] = jnp.where(
                    gy == n_gy - 1, jnp.where(lane < 32, turn(top, 32), turn(top, 64)), high
                )

        each_field(field)

    def conduct(z):
        for t in range(TILES + 2):
            cond[z, t] = 0.5 * jnp.exp(0.5 * jnp.tanh(q[5, z, t]))

    def minmod(a, b):
        return jnp.maximum(jnp.minimum(a, b), jnp.minimum(jnp.maximum(a, b), 0.0))

    def face(w, c, spread, d, left, right):
        return spread * c * d - w * jnp.where(w > 0.0, left, right)

    edge_low = (box == 0) & (col == 0)
    edge_high = (box == 3) & (col == 31)

    def x_next(values):
        return jnp.where(col == 31, sub(turn(values, 31), -1), turn(values, -1))

    def x_back(values):
        return jnp.where(col == 0, sub(turn(values, -31), 1), turn(values, 1))

    def y_next(values, later):
        return turn(jnp.where(lane < 32, later, values), -32)

    def y_back(values, earlier):
        return turn(jnp.where(lane >= 96, earlier, values), 32)

    def send_z():
        def pack_z(f, _):
            for t in range(1, TILES + 1):
                zsend[1, f, t - 1] = jnp.where(row < 4, q[f, 2, t], sub(q[f, 3, t], 4))
                zsend[0, f, t - 1] = jnp.where(row < 4, sub(q[f, 16, t], 4), q[f, 17, t])
            return 0

        lax.fori_loop(0, F, pack_z, 0)

        @pl.when(gx < n_gx - 1)
        def _():
            z_copy(0).start()

        @pl.when(gx > 0)
        def _():
            z_copy(1).start()

    def along_yx(z):
        conduct(z)
        for t in range(TILES + 1):
            u, c = q[1, z, t], cond[z, t]
            wy[t] = 0.125 * (u + y_next(u, q[1, z, t + 1]))
            cy[t] = c + y_next(c, cond[z, t + 1])
        for t in range(1, TILES + 1):
            u, c = q[0, z, t], cond[z, t]
            wx[t] = 0.125 * (u + jnp.where(edge_high, u, x_next(u)))
            cx[t] = c + jnp.where(edge_high, c, x_next(c))

        def differences(f):
            vals = [q[f, z, t] for t in range(TILES + 2)]
            for t in range(TILES + 2):
                dy[f, t] = y_next(vals[t], vals[min(t + 1, TILES + 1)]) - vals[t]
            for t in range(1, TILES + 1):
                dx[f, t] = jnp.where(edge_high, 0.0, x_next(vals[t]) - vals[t])

        def slopes(f):
            diffs = [dy[f, t] for t in range(TILES + 2)]
            for t in range(TILES + 2):
                hy[f, t] = 0.5 * minmod(y_back(diffs[t], diffs[max(t - 1, 0)]), diffs[t])
            for t in range(1, TILES + 1):
                d = dx[f, t]
                hx[f, t] = 0.5 * minmod(jnp.where(edge_low, 0.0, x_back(d)), d)

        def fluxes(f):
            spread = diff_ref[f]
            vals = [q[f, z, t] for t in range(TILES + 2)]
            halves = [hy[f, t] for t in range(TILES + 2)]
            rights = [v - h for v, h in zip(vals, halves)]
            for t in range(TILES + 1):
                ny[f, t] = face(
                    wy[t], cy[t], spread, dy[f, t], vals[t] + halves[t],
                    y_next(rights[t], rights[t + 1]),
                )
            for t in range(1, TILES + 1):
                v, half = vals[t], hx[f, t]
                right = jnp.where(edge_high, v, x_next(v - half))
                nx[f, t] = face(wx[t], cx[t], spread, dx[f, t], v + half, right)

        def sums(f):
            nets = [ny[f, t] for t in range(TILES + 1)]
            for t in range(1, TILES + 1):
                v, net = q[f, z, t], nx[f, t]
                total = v + (nets[t] - y_back(nets[t], nets[t - 1]))
                low = jnp.where(edge_low, -0.25 * q[0, z, t] * v, x_back(net))
                acc[f, z - 2, t - 1] = total + (net - low)

        for f in range(F):
            differences(f)
        for f in range(F):
            slopes(f)
        for f in range(F):
            fluxes(f)
        for f in range(F):
            sums(f)

    def update(k):
        fill_y(k)

        def plane(i, _):
            along_yx(k + 2 + 8 * i)
            return 0

        lax.fori_loop(0, 2, plane, 0)

    def step(k, _):
        @pl.when(k < CHUNKS)
        def _():
            gather(k)

        @pl.when(k == CHUNKS)
        def _():
            send_z()

        @pl.when(k >= AHEAD)
        def _():
            update(k - AHEAD)

        return 0

    lax.fori_loop(0, CHUNKS + AHEAD, step, 0)

    @pl.when(gx > 0)
    def _():
        z_copy(0).wait_recv()

    @pl.when(gx < n_gx - 1)
    def _():
        z_copy(1).wait_recv()

    def fill_z(f, _):
        for t in range(1, TILES + 1):
            lower = zrecv[0, f, t - 1]
            upper = zrecv[1, f, t - 1]
            z0, z1, z14, z15 = q[f, 2, t], q[f, 3, t], q[f, 16, t], q[f, 17, t]
            first = gx == 0
            last = gx == n_gx - 1
            q[f, 0, t] = jnp.where(row < 4, jnp.where(first, z0, lower), sub(z14, 4))
            q[f, 1, t] = jnp.where(row < 4, jnp.where(first, z0, sub(lower, 4)), sub(z15, 4))
            q[f, 18, t] = jnp.where(row < 4, sub(z0, 4), jnp.where(last, z15, sub(upper, 4)))
            q[f, 19, t] = jnp.where(row < 4, sub(z1, 4), jnp.where(last, z15, upper))
        return 0

    lax.fori_loop(0, F, fill_z, 0)

    conduct(1)
    conduct(18)

    def along_z(t, _):
        for i in range(17):
            wz[i] = 0.125 * (q[2, i + 1, t] + q[2, i + 2, t])
            cz[i] = cond[i + 1, t] + cond[i + 2, t]

        def field(f):
            spread = diff_ref[f]
            here = q[f, 1, t]
            d_low = here - q[f, 0, t]
            after = q[f, 2, t]
            d = after - here
            left = here + 0.5 * minmod(d_low, d)
            before = None
            for i in range(17):
                here = after
                after = q[f, i + 3, t]
                d_next = after - here
                half = 0.5 * minmod(d, d_next)
                net = face(wz[i], cz[i], spread, d, left, here - half)
                left = here + half
                d = d_next
                if i > 0:
                    total = acc[f, i - 1, t - 1] + (net - before)
                    start = pl.multiple_of((i - 1) * PLANE + (t - 1) * 128, 128)
                    out_ref[f, :, pl.ds(start, 128)] = total[:4]
                    out_ref[f, :, pl.ds(start + 16 * PLANE, 128)] = total[4:]
                before = net

        each_field(field)
        return 0

    lax.fori_loop(1, TILES + 1, along_z, 0)

    def finish(k, _):
        move(0, k).wait_send()
        move(1, k).wait_send()

        @pl.when(gy < n_gy - 1)
        def _():
            y_copy(0, k).wait_send()

        @pl.when(gy > 0)
        def _():
            y_copy(1, k).wait_send()

        return 0

    lax.fori_loop(0, CHUNKS, finish, 0)

    @pl.when(gx < n_gx - 1)
    def _():
        z_copy(0).wait_send()

    @pl.when(gx > 0)
    def _():
        z_copy(1).wait_send()


def solution(mesh):
    n_gx, n_gy = mesh.shape["gx"], mesh.shape["gy"]

    def local(old_state, old_owner, old_slot, diffusivity):
        def body(*refs):
            kernel(n_gx, n_gy, *refs)

        vmem = pltpu.VMEM
        dma = pltpu.SemaphoreType.DMA
        cells = old_state.shape[2]
        result = pl.pallas_call(
            body,
            out_shape=jax.ShapeDtypeStruct((F, CAP, cells), jnp.float32),
            in_specs=[
                pl.BlockSpec(memory_space=pltpu.SMEM),
                pl.BlockSpec(memory_space=pltpu.SMEM),
                pl.BlockSpec(memory_space=pl.ANY),
            ],
            out_specs=pl.BlockSpec(memory_space=pltpu.VMEM),
            scratch_shapes=[
                vmem((F, 8, cells), jnp.float32),
                vmem((2, CHUNKS, F, TILES, 8, 128), jnp.float32),
                vmem((2, CHUNKS, F, TILES, 8, 128), jnp.float32),
                vmem((F, 20, TILES + 2, 8, 128), jnp.float32),
                vmem((20, TILES + 2, 8, 128), jnp.float32),
                vmem((F, 16, TILES, 8, 128), jnp.float32),
                vmem((17, 8, 128), jnp.float32),
                vmem((17, 8, 128), jnp.float32),
                vmem((TILES + 2, 8, 128), jnp.float32),
                vmem((TILES + 2, 8, 128), jnp.float32),
                vmem((TILES + 2, 8, 128), jnp.float32),
                vmem((TILES + 2, 8, 128), jnp.float32),
                *[vmem((F, TILES + 2, 8, 128), jnp.float32) for _ in range(6)],
                vmem((2, F, TILES, 8, 128), jnp.float32),
                vmem((2, F, TILES, 8, 128), jnp.float32),
                vmem((2, CHUNKS, F, 8, 128), jnp.float32),
                vmem((2, CHUNKS, F, 8, 128), jnp.float32),
                dma((CHUNKS, 4)),
                dma((2, CHUNKS)),
                dma((2, CHUNKS)),
                dma((2,)),
                dma((2,)),
                dma((2, CHUNKS)),
                dma((2, CHUNKS)),
            ],
            compiler_params=pltpu.CompilerParams(
                collective_id=0, has_side_effects=True, vmem_limit_bytes=56 * 2**20
            ),
        )(old_owner, diffusivity, jnp.transpose(old_state, (1, 0, 2)))
        return jnp.transpose(result, (1, 0, 2))

    placed = (P(("gx", "gy"), None, None), P(), P(), P())
    return jax.shard_map(
        local, mesh=mesh, in_specs=placed, out_specs=P(("gx", "gy"), None, None), check_vma=False
    )
```

```python
import jax
import jax.numpy as jnp
from jax import lax
from jax.experimental import pallas as pl
from jax.experimental.pallas import tpu as pltpu
from jax.sharding import PartitionSpec as P

F = 6
CAP = 4
AHEAD = 3
LAG = 2
CHUNKS = 8
TILES = 8
PLANE = 1024
MESH = pl.DeviceIdType.MESH


def kernel(
    n_gx, n_gy, owner_ref, diff_ref, state_ref, out_ref,
    held, send, recv, q, cond, acc, wz, cz, wy, cy, wx, cx,
    dy, dx, hy, hx, ny, nx, zsend, zrecv, ysend, yrecv,
    in_sem, move_send, move_recv, z_send, z_recv, y_send, y_recv,
):
    gx = lax.axis_index("gx")
    gy = lax.axis_index("gy")
    count = n_gx * n_gy
    me = gx * n_gy + gy
    above = lax.rem(me + 1, count)
    below = lax.rem(me + count - 1, count)
    ring = ((above // n_gy, lax.rem(above, n_gy)), (below // n_gy, lax.rem(below, n_gy)))

    def in_copy(k, part):
        cells = pl.ds(pl.multiple_of((k + 8 * part) * PLANE, PLANE), PLANE)
        return pltpu.make_async_copy(
            state_ref.at[:, :, cells], held.at[:, :, cells], in_sem.at[k, part]
        )

    def start_in(k, _):
        for part in range(4):
            in_copy(k, part).start()
        return 0

    lax.fori_loop(0, CHUNKS, start_in, 0)

    barrier = pltpu.get_barrier_semaphore()
    for target in ring:
        pl.semaphore_signal(barrier, inc=1, device_id=target, device_id_type=MESH)

    @pl.when(gx > 0)
    def _():
        pl.semaphore_signal(barrier, inc=1, device_id=(gx - 1, gy), device_id_type=MESH)

    @pl.when(gx < n_gx - 1)
    def _():
        pl.semaphore_signal(barrier, inc=1, device_id=(gx + 1, gy), device_id_type=MESH)

    pl.semaphore_wait(
        barrier, 2 + (gx > 0).astype(jnp.int32) + (gx < n_gx - 1).astype(jnp.int32)
    )

    row = lax.broadcasted_iota(jnp.int32, (8, 128), 0)
    lane = lax.broadcasted_iota(jnp.int32, (8, 128), 1)
    box = row % 4
    col = lane % 32

    def sub(values, shift):
        return pltpu.roll(values, shift % 8, 0)

    def turn(values, shift):
        return pltpu.roll(values, shift % 128, 1)

    def each_field(work):
        def group(g, _):
            for f in range(F // 2):
                work(g * (F // 2) + f)
            return 0

        lax.fori_loop(0, 2, group, 0)

    def tile_of(f, k, part, t):
        start = pl.multiple_of((k + 8 * part) * PLANE + t * 128, 128)
        return held[f, :, pl.ds(start, 128)]

    def move(way, k):
        return pltpu.make_async_remote_copy(
            src_ref=send.at[way, k],
            dst_ref=recv.at[way, k],
            send_sem=move_send.at[way, k],
            recv_sem=move_recv.at[way, k],
            device_id=ring[way],
            device_id_type=MESH,
        )

    def start_move(k):
        move(0, k).start()
        move(1, k).start()

    def pack(k, _):
        for part in range(4):
            in_copy(k, part).wait()

        def field(f):
            for t in range(TILES):
                a, b, c, d = (tile_of(f, k, part, t) for part in range(4))
                a2, c6 = sub(a, 2), sub(c, 6)
                up = jnp.where(
                    row < 4, jnp.where(row < 2, a2, sub(b, 4)), jnp.where(row < 6, c6, d)
                )
                down = jnp.where(
                    row < 4, jnp.where(row < 2, b, a2), jnp.where(row < 6, sub(d, 4), c6)
                )
                send[0, k, f, t] = up
                send[1, k, f, t] = down

        each_field(field)
        @pl.when(k < AHEAD)
        def _():
            start_move(k)

        return 0

    lax.fori_loop(0, CHUNKS, pack, 0)

    owners = jnp.zeros((8, 128), jnp.int32)
    for c in range(CAP):
        owners = jnp.where(box == c, owner_ref[me * CAP + c], owners)
    kept = owners == me

    def y_copy(way, k):
        return pltpu.make_async_remote_copy(
            src_ref=ysend.at[way, k],
            dst_ref=yrecv.at[way, k],
            send_sem=y_send.at[way, k],
            recv_sem=y_recv.at[way, k],
            device_id=(gx, gy + 1) if way == 0 else (gx, gy - 1),
            device_id_type=MESH,
        )

    def z_copy(way):
        return pltpu.make_async_remote_copy(
            src_ref=zsend.at[way],
            dst_ref=zrecv.at[way],
            send_sem=z_send.at[way],
            recv_sem=z_recv.at[way],
            device_id=(gx + 1, gy) if way == 0 else (gx - 1, gy),
            device_id_type=MESH,
        )

    def gather(k):
        move(0, k).wait_recv()
        move(1, k).wait_recv()

        def field(f):
            for t in range(TILES):
                a, b, c, d = (tile_of(f, k, part, t) for part in range(4))
                up = recv[0, k, f, t]
                down = recv[1, k, f, t]
                first = jnp.where(
                    kept,
                    jnp.where(row < 4, sub(a, 6), sub(c, 2)),
                    jnp.where(box < 2, up, down),
                )
                second = jnp.where(
                    kept,
                    jnp.where(row < 4, sub(b, 6), sub(d, 2)),
                    jnp.where(box < 2, sub(up, 6), sub(down, 2)),
                )
                q[f, k + 2, t + 1] = first
                q[f, k + 10, t + 1] = second
                if t == 0:
                    ysend[1, k, f] = jnp.where(lane < 64, first, turn(second, 64))
                if t == TILES - 1:
                    ysend[0, k, f] = jnp.where(lane < 64, turn(second, 64), first)

        each_field(field)

        @pl.when(gy < n_gy - 1)
        def _():
            y_copy(0, k).start()

        @pl.when(gy > 0)
        def _():
            y_copy(1, k).start()

        @pl.when(k < CHUNKS - AHEAD)
        def _():
            start_move(k + AHEAD)

    def fill_y(k):
        @pl.when(gy > 0)
        def _():
            y_copy(0, k).wait_recv()

        @pl.when(gy < n_gy - 1)
        def _():
            y_copy(1, k).wait_recv()

        def field(f):
            lower = yrecv[0, k, f]
            upper = yrecv[1, k, f]
            for plane, low, high in (
                (k + 2, lower, upper), (k + 10, turn(lower, 64), turn(upper, 64))
            ):
                bottom = q[f, plane, 1]
                top = q[f, plane, TILES]
                q[f, plane, 0] = jnp.where(
                    gy == 0, jnp.where(lane < 96, turn(bottom, 64), turn(bottom, 96)), low
                )
                q[f, plane, TILES + 1] = jnp.where(
                    gy == n_gy - 1, jnp.where(lane < 32, turn(top, 32), turn(top, 64)), high
                )

        each_field(field)

    def conduct(z):
        for t in range(TILES + 2):
            cond[z, t] = 0.5 * jnp.exp(0.5 * jnp.tanh(q[5, z, t]))

    def minmod(a, b):
        return jnp.maximum(jnp.minimum(a, b), jnp.minimum(jnp.maximum(a, b), 0.0))

    def face(w, c, spread, d, left, right):
        return spread * c * d - w * jnp.where(w > 0.0, left, right)

    edge_low = (box == 0) & (col == 0)
    edge_high = (box == 3) & (col == 31)

    def x_next(values):
        return jnp.where(col == 31, sub(turn(values, 31), -1), turn(values, -1))

    def x_back(values):
        return jnp.where(col == 0, sub(turn(values, -31), 1), turn(values, 1))

    def y_next(values, later):
        return turn(jnp.where(lane < 32, later, values), -32)

    def y_back(values, earlier):
        return turn(jnp.where(lane >= 96, earlier, values), 32)

    def send_z():
        def pack_z(f, _):
            for t in range(1, TILES + 1):
                zsend[1, f, t - 1] = jnp.where(row < 4, q[f, 2, t], sub(q[f, 3, t], 4))
                zsend[0, f, t - 1] = jnp.where(row < 4, sub(q[f, 16, t], 4), q[f, 17, t])
            return 0

        lax.fori_loop(0, F, pack_z, 0)

        @pl.when(gx < n_gx - 1)
        def _():
            z_copy(0).start()

        @pl.when(gx > 0)
        def _():
            z_copy(1).start()

    def along_yx(z):
        conduct(z)
        for t in range(TILES + 1):
            u, c = q[1, z, t], cond[z, t]
            wy[t] = 0.125 * (u + y_next(u, q[1, z, t + 1]))
            cy[t] = c + y_next(c, cond[z, t + 1])
        for t in range(1, TILES + 1):
            u, c = q[0, z, t], cond[z, t]
            wx[t] = 0.125 * (u + jnp.where(edge_high, u, x_next(u)))
            cx[t] = c + jnp.where(edge_high, c, x_next(c))

        def differences(f):
            vals = [q[f, z, t] for t in range(TILES + 2)]
            for t in range(TILES + 2):
                dy[f, t] = y_next(vals[t], vals[min(t + 1, TILES + 1)]) - vals[t]
            for t in range(1, TILES + 1):
                dx[f, t] = jnp.where(edge_high, 0.0, x_next(vals[t]) - vals[t])

        def slopes(f):
            diffs = [dy[f, t] for t in range(TILES + 2)]
            for t in range(TILES + 2):
                hy[f, t] = 0.5 * minmod(y_back(diffs[t], diffs[max(t - 1, 0)]), diffs[t])
            for t in range(1, TILES + 1):
                d = dx[f, t]
                hx[f, t] = 0.5 * minmod(jnp.where(edge_low, 0.0, x_back(d)), d)

        def fluxes(f):
            spread = diff_ref[f]
            vals = [q[f, z, t] for t in range(TILES + 2)]
            halves = [hy[f, t] for t in range(TILES + 2)]
            rights = [v - h for v, h in zip(vals, halves)]
            for t in range(TILES + 1):
                ny[f, t] = face(
                    wy[t], cy[t], spread, dy[f, t], vals[t] + halves[t],
                    y_next(rights[t], rights[t + 1]),
                )
            for t in range(1, TILES + 1):
                v, half = vals[t], hx[f, t]
                right = jnp.where(edge_high, v, x_next(v - half))
                nx[f, t] = face(wx[t], cx[t], spread, dx[f, t], v + half, right)

        def sums(f):
            nets = [ny[f, t] for t in range(TILES + 1)]
            for t in range(1, TILES + 1):
                v, net = q[f, z, t], nx[f, t]
                total = v + (nets[t] - y_back(nets[t], nets[t - 1]))
                low = jnp.where(edge_low, -0.25 * q[0, z, t] * v, x_back(net))
                acc[f, z - 2, t - 1] = total + (net - low)

        for f in range(F):
            differences(f)
        for f in range(F):
            slopes(f)
        for f in range(F):
            fluxes(f)
        for f in range(F):
            sums(f)

    def update(k):
        fill_y(k)

        def plane(i, _):
            along_yx(k + 2 + 8 * i)
            return 0

        lax.fori_loop(0, 2, plane, 0)

    def step(k, _):
        @pl.when(k < CHUNKS)
        def _():
            gather(k)

        @pl.when(k == CHUNKS)
        def _():
            send_z()

        @pl.when(k >= LAG)
        def _():
            update(k - LAG)

        return 0

    lax.fori_loop(0, CHUNKS + LAG, step, 0)

    @pl.when(gx > 0)
    def _():
        z_copy(0).wait_recv()

    @pl.when(gx < n_gx - 1)
    def _():
        z_copy(1).wait_recv()

    def fill_z(f, _):
        for t in range(1, TILES + 1):
            lower = zrecv[0, f, t - 1]
            upper = zrecv[1, f, t - 1]
            z0, z1, z14, z15 = q[f, 2, t], q[f, 3, t], q[f, 16, t], q[f, 17, t]
            first = gx == 0
            last = gx == n_gx - 1
            q[f, 0, t] = jnp.where(row < 4, jnp.where(first, z0, lower), sub(z14, 4))
            q[f, 1, t] = jnp.where(row < 4, jnp.where(first, z0, sub(lower, 4)), sub(z15, 4))
            q[f, 18, t] = jnp.where(row < 4, sub(z0, 4), jnp.where(last, z15, sub(upper, 4)))
            q[f, 19, t] = jnp.where(row < 4, sub(z1, 4), jnp.where(last, z15, upper))
        return 0

    lax.fori_loop(0, F, fill_z, 0)

    conduct(1)
    conduct(18)

    def along_z(t, _):
        for i in range(17):
            wz[i] = 0.125 * (q[2, i + 1, t] + q[2, i + 2, t])
            cz[i] = cond[i + 1, t] + cond[i + 2, t]

        def field(f):
            spread = diff_ref[f]
            here = q[f, 1, t]
            d_low = here - q[f, 0, t]
            after = q[f, 2, t]
            d = after - here
            left = here + 0.5 * minmod(d_low, d)
            before = None
            for i in range(17):
                here = after
                after = q[f, i + 3, t]
                d_next = after - here
                half = 0.5 * minmod(d, d_next)
                net = face(wz[i], cz[i], spread, d, left, here - half)
                left = here + half
                d = d_next
                if i > 0:
                    total = acc[f, i - 1, t - 1] + (net - before)
                    start = pl.multiple_of((i - 1) * PLANE + (t - 1) * 128, 128)
                    out_ref[f, :, pl.ds(start, 128)] = total[:4]
                    out_ref[f, :, pl.ds(start + 16 * PLANE, 128)] = total[4:]
                before = net

        each_field(field)
        return 0

    lax.fori_loop(1, TILES + 1, along_z, 0)

    def finish(k, _):
        move(0, k).wait_send()
        move(1, k).wait_send()

        @pl.when(gy < n_gy - 1)
        def _():
            y_copy(0, k).wait_send()

        @pl.when(gy > 0)
        def _():
            y_copy(1, k).wait_send()

        return 0

    lax.fori_loop(0, CHUNKS, finish, 0)

    @pl.when(gx < n_gx - 1)
    def _():
        z_copy(0).wait_send()

    @pl.when(gx > 0)
    def _():
        z_copy(1).wait_send()


def solution(mesh):
    n_gx, n_gy = mesh.shape["gx"], mesh.shape["gy"]

    def local(old_state, old_owner, old_slot, diffusivity):
        def body(*refs):
            kernel(n_gx, n_gy, *refs)

        vmem = pltpu.VMEM
        dma = pltpu.SemaphoreType.DMA
        cells = old_state.shape[2]
        result = pl.pallas_call(
            body,
            out_shape=jax.ShapeDtypeStruct((F, CAP, cells), jnp.float32),
            in_specs=[
                pl.BlockSpec(memory_space=pltpu.SMEM),
                pl.BlockSpec(memory_space=pltpu.SMEM),
                pl.BlockSpec(memory_space=pl.ANY),
            ],
            out_specs=pl.BlockSpec(memory_space=pltpu.VMEM),
            scratch_shapes=[
                vmem((F, 8, cells), jnp.float32),
                vmem((2, CHUNKS, F, TILES, 8, 128), jnp.float32),
                vmem((2, CHUNKS, F, TILES, 8, 128), jnp.float32),
                vmem((F, 20, TILES + 2, 8, 128), jnp.float32),
                vmem((20, TILES + 2, 8, 128), jnp.float32),
                vmem((F, 16, TILES, 8, 128), jnp.float32),
                vmem((17, 8, 128), jnp.float32),
                vmem((17, 8, 128), jnp.float32),
                vmem((TILES + 2, 8, 128), jnp.float32),
                vmem((TILES + 2, 8, 128), jnp.float32),
                vmem((TILES + 2, 8, 128), jnp.float32),
                vmem((TILES + 2, 8, 128), jnp.float32),
                *[vmem((F, TILES + 2, 8, 128), jnp.float32) for _ in range(6)],
                vmem((2, F, TILES, 8, 128), jnp.float32),
                vmem((2, F, TILES, 8, 128), jnp.float32),
                vmem((2, CHUNKS, F, 8, 128), jnp.float32),
                vmem((2, CHUNKS, F, 8, 128), jnp.float32),
                dma((CHUNKS, 4)),
                dma((2, CHUNKS)),
                dma((2, CHUNKS)),
                dma((2,)),
                dma((2,)),
                dma((2, CHUNKS)),
                dma((2, CHUNKS)),
            ],
            compiler_params=pltpu.CompilerParams(
                collective_id=0, has_side_effects=True, vmem_limit_bytes=50 * 2**20
            ),
        )(old_owner, diffusivity, jnp.transpose(old_state, (1, 0, 2)))
        return jnp.transpose(result, (1, 0, 2))

    placed = (P(("gx", "gy"), None, None), P(), P(), P())
    return jax.shard_map(
        local, mesh=mesh, in_specs=placed, out_specs=P(("gx", "gy"), None, None), check_vma=False
    )
```
